512 devices in a mesh: col: 8 (over x, core), row: 64 (over y, z).
Axes of the slice: x: 4, y: 8, z: 8, core: 2. Of those that a mesh axis runs over, the one named last changes fastest.
Arguments:
- frames: bfloat16 [1536, 65536], P(('col', 'row')), as said below
- frame_order: int32 [1536], P('col'), may hold values from 0 to 191, as said below
Outputs:
- rotated: bfloat16 [1536, 65536], P('col', 'row')
The draws below stay inside these ranges and needn't reach their ends.
Inputs may be any that keep to these rules, and one draw needn't show every extreme that they name: `frame_order`: each aligned run of 192 entries is a permutation of 0 to 191. `frames`: frames have scales that differ from frame to frame and pixel to pixel.
All inputs are finite; a program needn't handle non-finite values.
Results may differ from the reference program's by a relative error of at most 0.015.
The reference program's roundings to bfloat16 on the way count: a program that leaves them out, or rounds other values in their place, can miss the bound.
Values may be sent and summed in bfloat16 or wider, within the bound.
No kernel may reach another device: no remote copies, remote signals or barrier semaphores. Data moves between devices by JAX's collectives and lax.ppermute only.
A program may use at most 64 MiB of HBM per device.

```python
import math
import jax
import jax.numpy as jnp
from jax import lax

BLOCK = 48
ROUNDS = 4
FR_DEV = 192
N = 1536
PIXELS = 65536


def draw_frames(key, part):
    key = jax.random.fold_in(key, 11)
    keys = jax.random.split(key, 3)
    frame_scale = jnp.exp(jax.random.uniform(keys[1], (N, 1), jnp.float32, math.log(0.5), math.log(5.0)))
    pixel_scale = jnp.exp(jax.random.uniform(keys[2], (1, PIXELS), jnp.float32, math.log(0.5), math.log(2.0)))
    values = jax.random.normal(keys[0], (N, PIXELS), jnp.float32) * frame_scale * pixel_scale
    return values.astype(jnp.bfloat16)


def draw_frame_order(key, part):
    key = jax.random.fold_in(key, 23)
    keys = jax.random.split(key, N // FR_DEV)
    orders = jax.vmap(lambda single: jax.random.permutation(single, FR_DEV))(keys)
    return orders.reshape(N).astype(jnp.int32)


def setup_inputs(seed: int = 0) -> dict:
    splits = jax.random.split(jax.random.key(seed), 3)
    frames = draw_frames(jax.random.fold_in(splits[2], 71), 0)
    frame_order = draw_frame_order(jax.random.fold_in(splits[2], 71), 0)
    return {"frames": frames, "frame_order": frame_order}


def rotation(gram):
    diag = jnp.diagonal(gram)
    gap = diag[None, :] - diag[:, None]
    total = diag[None, :] + diag[:, None]
    theta = gram * gap / (gap * gap + 4.0 * gram * gram + 0.01 * total * total)
    term = theta / 64.0
    result = jnp.eye(theta.shape[0], dtype=jnp.float32) + term
    power = term
    for order in range(2, 7):
        power = jnp.dot(power, term, precision=lax.Precision.HIGHEST) / float(order)
        result = result + power
    for square in range(6):
        result = jnp.dot(result, result, precision=lax.Precision.HIGHEST)
    return result


def one_pair(block):
    gram = jnp.dot(block, block.T, preferred_element_type=jnp.float32)
    rotor = rotation(gram).astype(jnp.bfloat16)
    return jnp.dot(rotor.T, block, preferred_element_type=jnp.float32).astype(jnp.bfloat16)


def reference(frames, frame_order):
    group = (jnp.arange(N, dtype=jnp.int32) // FR_DEV) * FR_DEV
    data = jnp.take(frames, (group + frame_order).astype(jnp.int32), axis=0)
    pairs = data.reshape(N // (2 * BLOCK), 2 * BLOCK, PIXELS)
    for step in range(ROUNDS):
        pairs = lax.map(one_pair, pairs)
        if step + 1 < ROUNDS:
            tops = pairs[:, :BLOCK]
            bottoms = pairs[:, BLOCK:]
            pairs = jnp.concatenate([jnp.roll(tops, 1, axis=0), jnp.roll(bottoms, -1, axis=0)], axis=1)
    return pairs.reshape(N, PIXELS)
```

```python
import functools

import jax
import jax.numpy as jnp
from jax import lax
from jax.experimental import pallas as pl
from jax.experimental.pallas import tpu as pltpu
from jax.sharding import PartitionSpec as P

BLOCK = 48
PAIR = 2 * BLOCK
LANES = 128
SPAN = 4
SLOTS = 15
CHUNK = LANES - PAIR

CARRIERS = [(c, s, t) for c in range(2) for s in range(SPAN) for t in range(s + 1, SPAN)]
CARRIERS += [(0, 0, 0), (0, 1, 1), (0, 2, 2)]
SPREAD = [(0, 3, 3), (1, 0, 0), (1, 1, 1), (1, 2, 2), (1, 3, 3)]


def passed_along(value, axis, steps):
    count = lax.axis_size(axis)
    pairs = [(source, (source + steps) % count) for source in range(count)]
    return lax.ppermute(value, axis, pairs)


def iota(shape, dim):
    return lax.broadcasted_iota(jnp.int32, shape, dim)


def mm(a, b):
    return jnp.dot(a, b, preferred_element_type=jnp.float32)


def mm_nt(a, b):
    return lax.dot_general(a, b, (((1,), (1,)), ((), ())), preferred_element_type=jnp.float32)


def halves(value):
    high = value.astype(jnp.bfloat16)
    low = (value - high.astype(jnp.float32)).astype(jnp.bfloat16)
    return high, low


def fill(rows_ref, own, prev, after, prev2, after2):
    width = own.shape[1]
    pieces = [
        [prev[0:PAIR], own[0:PAIR], after[0:PAIR], after2[...]],
        [prev2[...], prev[PAIR:], own[PAIR:], after[PAIR:]],
    ]
    for c in range(2):
        for s in range(SPAN):
            rows_ref[c, s, 0:PAIR, :] = pieces[c][s]
            rows_ref[c, s, PAIR:, :] = jnp.zeros((CHUNK, width), jnp.bfloat16)


def gram_kernel(own, prev, after, prev2, after2, packed, rows_ref):
    width = own.shape[1]
    fill(rows_ref, own, prev, after, prev2, after2)
    block = {}
    for c in range(2):
        for s in range(SPAN):
            right = rows_ref[c, s:SPAN].reshape((SPAN - s) * LANES, width)
            strip = mm_nt(rows_ref[c, s, 0:PAIR, :], right)
            for t in range(s, SPAN):
                block[c, s, t] = strip[:, (t - s) * LANES : (t - s + 1) * LANES]
    lane = iota((PAIR, LANES), 1)
    for k in range(SLOTS):
        extra = pltpu.roll(block[SPREAD[k // 3]], PAIR - CHUNK * (k % 3), 1)
        packed[k * PAIR : (k + 1) * PAIR, :] = jnp.where(lane < PAIR, block[CARRIERS[k]], extra)
    tail = packed.shape[0] - SLOTS * PAIR
    if tail:
        packed[SLOTS * PAIR :, :] = jnp.zeros((tail, LANES), jnp.float32)


def product(a, b):
    ah, al = a
    bh, bl = b
    wide = mm(jnp.concatenate([ah, al], axis=0), jnp.concatenate([bh, bl], axis=1))
    return wide[:LANES, :LANES] + (wide[LANES:, :LANES] + wide[:LANES, LANES:])


def turned_rotors(grams):
    shape = (LANES, LANES)
    row, lane = iota(shape, 0), iota(shape, 1)
    inside = (row < PAIR) & (lane < PAIR)
    eye = ((row == lane) & inside).astype(jnp.float32)
    terms = []
    for gram in grams:
        picked = gram * eye
        down = jnp.sum(picked, axis=1, keepdims=True)
        along = jnp.sum(picked, axis=0, keepdims=True)
        gap = along - down
        total = along + down
        bottom = gap * gap + 4.0 * gram * gram + 0.01 * total * total
        theta = gram * gap / jnp.where(inside, bottom, 1.0)
        terms.append(jnp.where(inside, theta, 0.0) * (-1.0 / 64.0))
    first = [halves(e) for e in terms]
    second = [product(a, a) for a in first]
    third = [product(halves(e2), a) for e2, a in zip(second, first)]
    result = []
    for e, e2, e3 in zip(terms, second, third):
        rest = e * (1.0 / 24.0) + e2 * (1.0 / 120.0) + e3 * (1.0 / 720.0)
        result.append(e + e2 * 0.5 + e3 * (1.0 / 6.0) + product(halves(e3), halves(rest)))
    for _ in range(6):
        split = [halves(d) for d in result]
        result = [2.0 * d + product(a, a) for d, a in zip(result, split)]
    return [(d + eye).astype(jnp.bfloat16) for d in result]


def rounds_kernel(packed, own, prev, after, prev2, after2, out, rows_ref):
    width = own.shape[1]
    fill(rows_ref, own, prev, after, prev2, after2)
    lane = iota((PAIR, LANES), 1)
    floor = jnp.zeros((CHUNK, LANES), jnp.float32)
    gram = {}
    slot = [packed[k * PAIR : (k + 1) * PAIR, :] for k in range(SLOTS)]
    for k, name in enumerate(CARRIERS):
        gram[name] = jnp.concatenate([jnp.where(lane < PAIR, slot[k], 0.0), floor], axis=0)
    for m, name in enumerate(SPREAD):
        value = jnp.zeros((PAIR, LANES), jnp.float32)
        for j in range(3):
            moved = pltpu.roll(slot[3 * m + j], (CHUNK * j - PAIR) % LANES, 1)
            value = jnp.where((lane >= CHUNK * j) & (lane < CHUNK * (j + 1)), moved, value)
        gram[name] = jnp.concatenate([value, floor], axis=0)
    top_lane = iota((LANES, LANES), 1) < BLOCK
    top_half = iota((BLOCK, LANES), 1) < BLOCK
    count = SPAN
    while True:
        names = [(c, s) for c in range(2) for s in range(count)]
        turned = dict(zip(names, turned_rotors([gram[c, s, s] for c, s in names])))
        if count == 1:
            break
        following = {}
        for c in range(2):
            right = {}
            for t in range(count):
                stack = []
                for s in range(t + 1):
                    stack += halves(gram[c, s, t])
                both = mm_nt(jnp.concatenate(stack, axis=0), turned[c, t])
                for s in range(t + 1):
                    at = 2 * s * LANES
                    right[s, t] = both[at : at + LANES] + both[at + LANES : at + 2 * LANES]

            def left(rows, value):
                high, low = halves(value)
                both = mm(rows, jnp.concatenate([high, low], axis=1))
                return both[:, :LANES] + both[:, LANES:]

            for i in range(count - 1):
                upper = turned[c, i][0:BLOCK]
                lower = turned[c, i + 1][BLOCK:PAIR]
                for j in range(i, count - 1):
                    top = left(upper, jnp.where(top_lane, right[i, j], right[i, j + 1]))
                    if i == j:
                        bottom = left(lower, right[i + 1, j + 1])
                        padded = jnp.concatenate(
                            [top, jnp.zeros((LANES - BLOCK, LANES), jnp.float32)], axis=0
                        )
                        bottom = jnp.where(top_half, padded.T[BLOCK:PAIR], bottom)
                    else:
                        bottom = left(lower, jnp.where(top_lane, right[i + 1, j], right[i + 1, j + 1]))
                    following[c, i, j] = jnp.concatenate([top, bottom, floor], axis=0)
            for i in range(count):
                old = rows_ref[c, i]
                if i > 0:
                    lower = turned[c, i][BLOCK:PAIR]
                    rows_ref[c, i - 1, BLOCK:PAIR, :] = mm(lower, old).astype(jnp.bfloat16)
                if i < count - 1:
                    upper = turned[c, i][0:BLOCK]
                    rows_ref[c, i, 0:BLOCK, :] = mm(upper, old).astype(jnp.bfloat16)
        gram = following
        count -= 1
    for c in range(2):
        last = mm(turned[c, 0][0:PAIR], rows_ref[c, 0]).astype(jnp.bfloat16)
        out[(1 - c) * PAIR : (2 - c) * PAIR, :] = last


def on_device(frames, frame_order):
    row_count = lax.axis_size("row")
    width = frames.shape[1] // row_count
    arrived = lax.all_to_all(frames, "row", split_axis=1, concat_axis=0, tiled=True)
    own = jnp.take(arrived, frame_order, axis=0)
    prev = passed_along(own, "col", 1)
    after = passed_along(own, "col", -1)
    prev2 = passed_along(own[PAIR:], "col", 2)
    after2 = passed_along(own[:PAIR], "col", -2)
    held = (own, prev, after, prev2, after2)
    share = -(-SLOTS * PAIR // (8 * row_count)) * 8
    limit = pltpu.CompilerParams(vmem_limit_bytes=48 * 1024 * 1024)
    scratch = [pltpu.VMEM((2, SPAN, LANES, width), jnp.bfloat16)]
    packed = pl.pallas_call(
        gram_kernel,
        out_shape=jax.ShapeDtypeStruct((share * row_count, LANES), jnp.float32),
        scratch_shapes=scratch,
        compiler_params=limit,
        name="grams",
    )(*held)
    parts = packed.reshape(row_count, share, LANES)
    parts = lax.all_to_all(parts, "row", split_axis=0, concat_axis=0, tiled=True)
    summed = jnp.sum(parts, axis=0)
    copies = jnp.broadcast_to(summed[None], (row_count, share, LANES))
    whole = lax.all_to_all(copies, "row", split_axis=0, concat_axis=0, tiled=True)
    return pl.pallas_call(
        rounds_kernel,
        out_shape=jax.ShapeDtypeStruct((4 * BLOCK, width), jnp.bfloat16),
        scratch_shapes=scratch,
        compiler_params=limit,
        name="rounds",
    )(whole.reshape(row_count * share, LANES), *held)


def solution(mesh):
    placed = (P(("col", "row"), None), P("col"))
    return jax.shard_map(
        on_device, mesh=mesh, in_specs=placed, out_specs=P("col", "row"), check_vma=False
    )
```

```python
import jax
import jax.numpy as jnp
from jax import lax
from jax.experimental import pallas as pl
from jax.experimental.pallas import tpu as pltpu
from jax.sharding import PartitionSpec as P

BLOCK = 48
PAIR = 2 * BLOCK
LANES = 128
ROUNDS = 4
SPAN = 5
CHUNK = LANES - PAIR

BLOCKS = [(s, t) for s in range(SPAN) for t in range(s + 1, min(s + ROUNDS, SPAN))]
BLOCKS += [(s, s) for s in range(SPAN)]
SLOTS = 10
CARRIERS, SPREAD, LAST = BLOCKS[:SLOTS], BLOCKS[SLOTS : SLOTS + 3], BLOCKS[SLOTS + 3]
USED = SLOTS * PAIR + BLOCK


def iota(shape, dim):
    return lax.broadcasted_iota(jnp.int32, shape, dim)


def mm(a, b):
    return jnp.dot(a, b, preferred_element_type=jnp.float32)


def mm_nt(a, b):
    return lax.dot_general(a, b, (((1,), (1,)), ((), ())), preferred_element_type=jnp.float32)


def halves(value):
    high = value.astype(jnp.bfloat16)
    low = (value - high.astype(jnp.float32)).astype(jnp.bfloat16)
    return high, low


def shifted(value, lanes):
    return pltpu.roll(value, lanes % LANES, 1)


def fill(rows_ref, core, mine, partner, across, left, right):
    first = core[0] == 0
    pieces = [
        left[...],
        jnp.where(first, across[...], partner[...]),
        mine[...],
        jnp.where(first, partner[...], across[...]),
        right[...],
    ]
    for s in range(SPAN):
        rows_ref[s, 0:PAIR, :] = pieces[s]
        rows_ref[s, PAIR:, :] = jnp.zeros((CHUNK, mine.shape[1]), jnp.bfloat16)


def gram_kernel(core, mine, partner, across, left, right, packed, rows_ref):
    width = mine.shape[1]
    fill(rows_ref, core, mine, partner, across, left, right)
    block = {}
    for s in range(SPAN):
        end = min(s + ROUNDS, SPAN)
        others = rows_ref[s:end].reshape((end - s) * LANES, width)
        strip = mm_nt(rows_ref[s, 0:PAIR, :], others)
        for t in range(s, end):
            block[s, t] = strip[:, (t - s) * LANES : (t - s + 1) * LANES]
    lane = iota((PAIR, LANES), 1)
    last = block[LAST]
    for k in range(SLOTS):
        extra = shifted(block[SPREAD[k // 3]], PAIR - CHUNK * (k % 3)) if k < 9 else shifted(last, PAIR)
        packed[k * PAIR : (k + 1) * PAIR, :] = jnp.where(lane < PAIR, block[CARRIERS[k]], extra)
    packed[SLOTS * PAIR : USED, :] = jnp.where(
        lane[:BLOCK] < LANES // 2, shifted(last[:BLOCK], -CHUNK), shifted(last[BLOCK:], CHUNK)
    )
    tail = packed.shape[0] - USED
    if tail:
        packed[USED:, :] = jnp.zeros((tail, LANES), jnp.float32)


def unpacked(packed):
    lane = iota((PAIR, LANES), 1)
    floor = jnp.zeros((CHUNK, LANES), jnp.float32)
    slot = [packed[k * PAIR : (k + 1) * PAIR, :] for k in range(SLOTS)]
    gram = {}
    for k, name in enumerate(CARRIERS):
        gram[name] = jnp.where(lane < PAIR, slot[k], 0.0)
    for m, name in enumerate(SPREAD):
        value = jnp.zeros((PAIR, LANES), jnp.float32)
        for j in range(3):
            here = (lane >= CHUNK * j) & (lane < CHUNK * (j + 1))
            value = jnp.where(here, shifted(slot[3 * m + j], CHUNK * j - PAIR), value)
        gram[name] = value
    rest = packed[SLOTS * PAIR : USED, :]
    sides = jnp.concatenate([shifted(rest, CHUNK), shifted(rest, -CHUNK)], axis=0)
    value = jnp.where(lane < CHUNK, shifted(slot[SLOTS - 1], -PAIR), sides)
    gram[LAST] = jnp.where(lane < PAIR, value, 0.0)
    return {name: jnp.concatenate([value, floor], axis=0) for name, value in gram.items()}


def product(a, b):
    ah, al = a
    bh, bl = b
    wide = mm(jnp.concatenate([ah, al], axis=0), jnp.concatenate([bh, bl], axis=1))
    return wide[:LANES, :LANES] + (wide[LANES:, :LANES] + wide[:LANES, LANES:])


def turned_rotors(grams):
    shape = (LANES, LANES)
    row, lane = iota(shape, 0), iota(shape, 1)
    inside = (row < PAIR) & (lane < PAIR)
    eye = ((row == lane) & inside).astype(jnp.float32)
    terms = []
    for gram in grams:
        picked = gram * eye
        down = jnp.sum(picked, axis=1, keepdims=True)
        along = jnp.sum(picked, axis=0, keepdims=True)
        gap = along - down
        total = along + down
        bottom = gap * gap + 4.0 * gram * gram + 0.01 * total * total
        theta = gram * gap / jnp.where(inside, bottom, 1.0)
        terms.append(jnp.where(inside, theta, 0.0) * (-1.0 / 64.0))
    first = [halves(e) for e in terms]
    second = [product(a, a) for a in first]
    third = [product(halves(e2), a) for e2, a in zip(second, first)]
    result = []
    for e, e2, e3 in zip(terms, second, third):
        rest = e * (1.0 / 24.0) + e2 * (1.0 / 120.0) + e3 * (1.0 / 720.0)
        result.append(e + e2 * 0.5 + e3 * (1.0 / 6.0) + product(halves(e3), halves(rest)))
    for _ in range(6):
        split = [halves(d) for d in result]
        result = [2.0 * d + product(a, a) for d, a in zip(result, split)]
    return [(d + eye).astype(jnp.bfloat16) for d in result]


def turned_from_left(rows, value):
    high, low = halves(value)
    both = mm(rows, jnp.concatenate([high, low], axis=1))
    return both[:, :LANES] + both[:, LANES:]


def next_grams(gram, turned, count, reach):
    top_lane = iota((LANES, LANES), 1) < BLOCK
    top_half = iota((BLOCK, LANES), 1) < BLOCK
    floor = jnp.zeros((CHUNK, LANES), jnp.float32)
    right = {}
    for t in range(count):
        low = max(0, t - reach)
        stack = []
        for s in range(low, t + 1):
            stack += halves(gram[s, t])
        both = mm_nt(jnp.concatenate(stack, axis=0), turned[t])
        for s in range(low, t + 1):
            at = 2 * (s - low) * LANES
            right[s, t] = both[at : at + LANES] + both[at + LANES : at + 2 * LANES]
    following = {}
    for i in range(count - 1):
        upper, lower = turned[i][0:BLOCK], turned[i + 1][BLOCK:PAIR]
        for j in range(i, min(i + reach, count - 1)):
            top = turned_from_left(upper, jnp.where(top_lane, right[i, j], right[i, j + 1]))
            if i == j:
                bottom = turned_from_left(lower, right[i + 1, j + 1])
                empty = jnp.zeros((LANES - BLOCK, LANES), jnp.float32)
                mirrored = jnp.concatenate([top, empty], axis=0).T[BLOCK:PAIR]
                bottom = jnp.where(top_half, mirrored, bottom)
            else:
                bottom = turned_from_left(lower, jnp.where(top_lane, right[i + 1, j], right[i + 1, j + 1]))
            following[i, j] = jnp.concatenate([top, bottom, floor], axis=0)
    return following


def rounds_kernel(core, packed, mine, partner, across, left, right, kept, sent, rows_ref):
    fill(rows_ref, core, mine, partner, across, left, right)
    gram = unpacked(packed)
    for step in range(ROUNDS):
        count, reach = SPAN - step, ROUNDS - 1 - step
        turned = turned_rotors([gram[s, s] for s in range(count)])
        if reach == 0:
            break
        gram = next_grams(gram, turned, count, reach)
        for i in range(count):
            old = rows_ref[i]
            if i > 0:
                lower = turned[i][BLOCK:PAIR]
                rows_ref[i - 1, BLOCK:PAIR, :] = mm(lower, old).astype(jnp.bfloat16)
            if i < count - 1:
                upper = turned[i][0:BLOCK]
                rows_ref[i, 0:BLOCK, :] = mm(upper, old).astype(jnp.bfloat16)
    first = core[0] == 0
    ends = [mm(turned[i][0:PAIR], rows_ref[i]).astype(jnp.bfloat16) for i in range(2)]
    kept[...] = jnp.where(first, ends[0], ends[1])
    sent[...] = jnp.where(first, ends[1], ends[0])


def passed(value, where):
    count = lax.axis_size("col")
    return lax.ppermute(value, "col", [(source, where(source) % count) for source in range(count)])


def on_device(frames, frame_order):
    row_count = lax.axis_size("row")
    width = frames.shape[1] // row_count
    core = lax.axis_index("col") % 2
    arrived = lax.all_to_all(frames, "row", split_axis=1, concat_axis=0, tiled=True)
    order = jnp.where(core == 0, jnp.roll(frame_order, PAIR), frame_order)
    mine = jnp.take(arrived, order[:PAIR], axis=0)
    other = jnp.take(arrived, order[PAIR:], axis=0)
    partner = passed(other, lambda c: c ^ 1)
    across = passed(other, lambda c: c - 1 if c % 2 == 0 else c + 1)
    left = passed(mine, lambda c: c + 2)
    right = passed(mine, lambda c: c - 2)
    held = (mine, partner, across, left, right)
    chosen = core.astype(jnp.int32).reshape(1)
    share = -(-USED // (8 * row_count)) * 8
    limit = pltpu.CompilerParams(vmem_limit_bytes=48 * 1024 * 1024)
    scratch = [pltpu.VMEM((SPAN, LANES, width), jnp.bfloat16)]
    scalar = pl.BlockSpec(memory_space=pltpu.SMEM)
    vector = pl.BlockSpec(memory_space=pltpu.VMEM)
    packed = pl.pallas_call(
        gram_kernel,
        out_shape=jax.ShapeDtypeStruct((share * row_count, LANES), jnp.float32),
        in_specs=[scalar] + [vector] * 5,
        scratch_shapes=scratch,
        compiler_params=limit,
        name="grams",
    )(chosen, *held)
    parts = packed.reshape(row_count, share, LANES)
    parts = lax.all_to_all(parts, "row", split_axis=0, concat_axis=0, tiled=True)
    summed = jnp.sum(parts, axis=0)
    copies = jnp.broadcast_to(summed[None], (row_count, share, LANES))
    whole = lax.all_to_all(copies, "row", split_axis=0, concat_axis=0, tiled=True)
    pair = jax.ShapeDtypeStruct((PAIR, width), jnp.bfloat16)
    kept, sent = pl.pallas_call(
        rounds_kernel,
        out_shape=(pair, pair),
        in_specs=[scalar] + [vector] * 6,
        scratch_shapes=scratch,
        compiler_params=limit,
        name="rounds",
    )(chosen, whole.reshape(row_count * share, LANES), *held)
    got = passed(sent, lambda c: c ^ 1)
    upper = jnp.where(core == 0, kept, got)
    lower = jnp.where(core == 0, got, kept)
    return jnp.concatenate([upper, lower], axis=0)


def solution(mesh):
    placed = (P(("col", "row"), None), P("col"))
    return jax.shard_map(
        on_device, mesh=mesh, in_specs=placed, out_specs=P("col", "row"), check_vma=False
    )
```

```python
import jax
import jax.numpy as jnp
from jax import lax
from jax.experimental import pallas as pl
from jax.experimental.pallas import tpu as pltpu
from jax.sharding import PartitionSpec as P

BLOCK = 48
PAIR = 2 * BLOCK
LANES = 128
ROUNDS = 4
SPAN = 5
CHUNK = LANES - PAIR

BLOCKS = [(s, t) for s in range(SPAN) for t in range(s + 1, min(s + ROUNDS, SPAN))]
BLOCKS += [(s, s) for s in range(SPAN)]
SLOTS = 10
CARRIERS, SPREAD, LAST = BLOCKS[:SLOTS], BLOCKS[SLOTS : SLOTS + 3], BLOCKS[SLOTS + 3]
USED = SLOTS * PAIR + BLOCK


def iota(shape, dim):
    return lax.broadcasted_iota(jnp.int32, shape, dim)


def mm(a, b):
    return jnp.dot(a, b, preferred_element_type=jnp.float32)


def mm_nt(a, b):
    return lax.dot_general(a, b, (((1,), (1,)), ((), ())), preferred_element_type=jnp.float32)


def halves(value):
    high = value.astype(jnp.bfloat16)
    low = (value - high.astype(jnp.float32)).astype(jnp.bfloat16)
    return high, low


def shifted(value, lanes):
    return pltpu.roll(value, lanes % LANES, 1)


def fill(rows_ref, core, mine, partner, near, far):
    first = core[0] == 0
    pieces = [
        jnp.where(first, near[0:PAIR], far[...]),
        jnp.where(first, near[PAIR:], partner[...]),
        mine[...],
        jnp.where(first, partner[...], near[PAIR:]),
        jnp.where(first, far[...], near[0:PAIR]),
    ]
    for s in range(SPAN):
        rows_ref[s, 0:PAIR, :] = pieces[s]
        rows_ref[s, PAIR:, :] = jnp.zeros((CHUNK, mine.shape[1]), jnp.bfloat16)


def gram_kernel(core, mine, partner, near, far, packed, rows_ref):
    width = mine.shape[1]
    fill(rows_ref, core, mine, partner, near, far)
    block = {}
    for s in range(SPAN):
        end = min(s + ROUNDS, SPAN)
        others = rows_ref[s:end].reshape((end - s) * LANES, width)
        strip = mm_nt(rows_ref[s, 0:PAIR, :], others)
        for t in range(s, end):
            block[s, t] = strip[:, (t - s) * LANES : (t - s + 1) * LANES]
    lane = iota((PAIR, LANES), 1)
    last = block[LAST]
    for k in range(SLOTS):
        extra = shifted(block[SPREAD[k // 3]], PAIR - CHUNK * (k % 3)) if k < 9 else shifted(last, PAIR)
        packed[k * PAIR : (k + 1) * PAIR, :] = jnp.where(lane < PAIR, block[CARRIERS[k]], extra)
    packed[SLOTS * PAIR : USED, :] = jnp.where(
        lane[:BLOCK] < LANES // 2, shifted(last[:BLOCK], -CHUNK), shifted(last[BLOCK:], CHUNK)
    )
    tail = packed.shape[0] - USED
    if tail:
        packed[USED:, :] = jnp.zeros((tail, LANES), jnp.float32)


def unpacked(packed):
    lane = iota((PAIR, LANES), 1)
    floor = jnp.zeros((CHUNK, LANES), jnp.float32)
    slot = [packed[k * PAIR : (k + 1) * PAIR, :] for k in range(SLOTS)]
    gram = {}
    for k, name in enumerate(CARRIERS):
        gram[name] = jnp.where(lane < PAIR, slot[k], 0.0)
    for m, name in enumerate(SPREAD):
        value = jnp.zeros((PAIR, LANES), jnp.float32)
        for j in range(3):
            here = (lane >= CHUNK * j) & (lane < CHUNK * (j + 1))
            value = jnp.where(here, shifted(slot[3 * m + j], CHUNK * j - PAIR), value)
        gram[name] = value
    rest = packed[SLOTS * PAIR : USED, :]
    sides = jnp.concatenate([shifted(rest, CHUNK), shifted(rest, -CHUNK)], axis=0)
    value = jnp.where(lane < CHUNK, shifted(slot[SLOTS - 1], -PAIR), sides)
    gram[LAST] = jnp.where(lane < PAIR, value, 0.0)
    return {name: jnp.concatenate([value, floor], axis=0) for name, value in gram.items()}


def product(a, b):
    ah, al = a
    bh, bl = b
    wide = mm(jnp.concatenate([ah, al], axis=0), jnp.concatenate([bh, bl], axis=1))
    return wide[:LANES, :LANES] + (wide[LANES:, :LANES] + wide[:LANES, LANES:])


def turned_rotors(grams):
    shape = (LANES, LANES)
    row, lane = iota(shape, 0), iota(shape, 1)
    inside = (row < PAIR) & (lane < PAIR)
    eye = ((row == lane) & inside).astype(jnp.float32)
    terms = []
    for gram in grams:
        picked = gram * eye
        down = jnp.sum(picked, axis=1, keepdims=True)
        along = jnp.sum(picked, axis=0, keepdims=True)
        gap = along - down
        total = along + down
        bottom = gap * gap + 4.0 * gram * gram + 0.01 * total * total
        theta = gram * gap / jnp.where(inside, bottom, 1.0)
        terms.append(jnp.where(inside, theta, 0.0) * (-1.0 / 64.0))
    first = [halves(e) for e in terms]
    second = [product(a, a) for a in first]
    third = [product(halves(e2), a) for e2, a in zip(second, first)]
    result = []
    for e, e2, e3 in zip(terms, second, third):
        rest = e * (1.0 / 24.0) + e2 * (1.0 / 120.0) + e3 * (1.0 / 720.0)
        result.append(e + e2 * 0.5 + e3 * (1.0 / 6.0) + product(halves(e3), halves(rest)))
    for _ in range(6):
        split = [halves(d) for d in result]
        result = [2.0 * d + product(a, a) for d, a in zip(result, split)]
    return [(d + eye).astype(jnp.bfloat16) for d in result]


def turned_from_left(rows, value):
    high, low = halves(value)
    both = mm(rows, jnp.concatenate([high, low], axis=1))
    return both[:, :LANES] + both[:, LANES:]


def next_grams(gram, turned, count, reach):
    top_lane = iota((LANES, LANES), 1) < BLOCK
    top_half = iota((BLOCK, LANES), 1) < BLOCK
    floor = jnp.zeros((CHUNK, LANES), jnp.float32)
    right = {}
    for t in range(count):
        low = max(0, t - reach)
        stack = []
        for s in range(low, t + 1):
            stack += halves(gram[s, t])
        both = mm_nt(jnp.concatenate(stack, axis=0), turned[t])
        for s in range(low, t + 1):
            at = 2 * (s - low) * LANES
            right[s, t] = both[at : at + LANES] + both[at + LANES : at + 2 * LANES]
    following = {}
    for i in range(count - 1):
        upper, lower = turned[i][0:BLOCK], turned[i + 1][BLOCK:PAIR]
        for j in range(i, min(i + reach, count - 1)):
            top = turned_from_left(upper, jnp.where(top_lane, right[i, j], right[i, j + 1]))
            if i == j:
                bottom = turned_from_left(lower, right[i + 1, j + 1])
                empty = jnp.zeros((LANES - BLOCK, LANES), jnp.float32)
                mirrored = jnp.concatenate([top, empty], axis=0).T[BLOCK:PAIR]
                bottom = jnp.where(top_half, mirrored, bottom)
            else:
                bottom = turned_from_left(lower, jnp.where(top_lane, right[i + 1, j], right[i + 1, j + 1]))
            following[i, j] = jnp.concatenate([top, bottom, floor], axis=0)
    return following


def rounds_kernel(core, packed, mine, partner, near, far, out, sent, rows_ref):
    fill(rows_ref, core, mine, partner, near, far)
    gram = unpacked(packed)
    for step in range(ROUNDS):
        count, reach = SPAN - step, ROUNDS - 1 - step
        turned = turned_rotors([gram[s, s] for s in range(count)])
        if reach == 0:
            break
        gram = next_grams(gram, turned, count, reach)
        for i in range(count):
            old = rows_ref[i]
            if i > 0:
                lower = turned[i][BLOCK:PAIR]
                rows_ref[i - 1, BLOCK:PAIR, :] = mm(lower, old).astype(jnp.bfloat16)
            if i < count - 1:
                upper = turned[i][0:BLOCK]
                rows_ref[i, 0:BLOCK, :] = mm(upper, old).astype(jnp.bfloat16)
    first = core[0] == 0
    ends = [mm(turned[i][0:PAIR], rows_ref[i]).astype(jnp.bfloat16) for i in range(2)]
    out[pl.ds(pl.multiple_of(core[0] * PAIR, PAIR), PAIR), :] = jnp.where(first, ends[0], ends[1])
    sent[...] = jnp.where(first, ends[1], ends[0])


def passed(value, where):
    count = lax.axis_size("col")
    return lax.ppermute(value, "col", [(source, where(source) % count) for source in range(count)])


def on_device(frames, frame_order):
    row_count = lax.axis_size("row")
    width = frames.shape[1] // row_count
    core = lax.axis_index("col") % 2
    arrived = lax.all_to_all(frames, "row", split_axis=1, concat_axis=0, tiled=True)
    order = jnp.where(core == 0, jnp.roll(frame_order, PAIR), frame_order)
    picks = (order[:, None] == iota((1, order.shape[0]), 1)).astype(jnp.bfloat16)
    mine = mm(picks[:PAIR], arrived).astype(jnp.bfloat16)
    other = mm(picks[PAIR:], arrived).astype(jnp.bfloat16)
    partner = passed(other, lambda c: c ^ 1)
    far = passed(mine, lambda c: c - 2 if c % 2 == 0 else c + 2)
    near = passed(jnp.concatenate([mine, partner], axis=0), lambda c: c + 2 if c % 2 == 0 else c - 2)
    held = (mine, partner, near, far)
    chosen = core.astype(jnp.int32).reshape(1)
    share = -(-USED // (8 * row_count)) * 8
    limit = pltpu.CompilerParams(vmem_limit_bytes=48 * 1024 * 1024)
    scratch = [pltpu.VMEM((SPAN, LANES, width), jnp.bfloat16)]
    scalar = pl.BlockSpec(memory_space=pltpu.SMEM)
    vector = pl.BlockSpec(memory_space=pltpu.VMEM)
    packed = pl.pallas_call(
        gram_kernel,
        out_shape=jax.ShapeDtypeStruct((share * row_count, LANES), jnp.float32),
        in_specs=[scalar] + [vector] * 4,
        scratch_shapes=scratch,
        compiler_params=limit,
        name="grams",
    )(chosen, *held)
    parts = packed.reshape(row_count, share, LANES)
    parts = lax.all_to_all(parts, "row", split_axis=0, concat_axis=0, tiled=True)
    summed = jnp.sum(parts, axis=0)
    copies = jnp.broadcast_to(summed[None], (row_count, share, LANES))
    whole = lax.all_to_all(copies, "row", split_axis=0, concat_axis=0, tiled=True)
    half, sent = pl.pallas_call(
        rounds_kernel,
        out_shape=tuple(jax.ShapeDtypeStruct((rows, width), jnp.bfloat16) for rows in (2 * PAIR, PAIR)),
        in_specs=[scalar] + [vector] * 5,
        scratch_shapes=scratch,
        compiler_params=limit,
        name="rounds",
    )(chosen, whole.reshape(row_count * share, LANES), *held)
    got = passed(sent, lambda c: c ^ 1)
    return lax.dynamic_update_slice(half, got, ((1 - core) * PAIR, 0))


def solution(mesh):
    placed = (P(("col", "row"), None), P("col"))
    return jax.shard_map(
        on_device, mesh=mesh, in_specs=placed, out_specs=P("col", "row"), check_vma=False
    )
```

```python
import jax
import jax.numpy as jnp
from jax import lax
from jax.experimental import pallas as pl
from jax.experimental.pallas import tpu as pltpu
from jax.sharding import PartitionSpec as P

BLOCK = 48
PAIR = 2 * BLOCK
LANES = 128
ROUNDS = 4
SPAN = 5
CHUNK = LANES - PAIR

BLOCKS = [(s, t) for s in range(SPAN) for t in range(s + 1, min(s + ROUNDS, SPAN))]
BLOCKS += [(s, s) for s in range(SPAN)]
SLOTS = 10
CARRIERS, SPREAD, LAST = BLOCKS[:SLOTS], BLOCKS[SLOTS : SLOTS + 3], BLOCKS[SLOTS + 3]
USED = SLOTS * PAIR + BLOCK
EXTRA = 16


def iota(shape, dim):
    return lax.broadcasted_iota(jnp.int32, shape, dim)


def mm(a, b):
    return jnp.dot(a, b, preferred_element_type=jnp.float32)


def mm_nt(a, b):
    return lax.dot_general(a, b, (((1,), (1,)), ((), ())), preferred_element_type=jnp.float32)


def halves(value):
    high = value.astype(jnp.bfloat16)
    low = (value - high.astype(jnp.float32)).astype(jnp.bfloat16)
    return high, low


def shifted(value, lanes):
    return pltpu.roll(value, lanes % LANES, 1)


def fill(rows_ref, core, mine, partner, near, far):
    first = core[0] == 0
    pieces = [
        jnp.where(first, near[0:PAIR], far[...]),
        jnp.where(first, near[PAIR:], partner[...]),
        mine[...],
        jnp.where(first, partner[...], near[PAIR:]),
        jnp.where(first, far[...], near[0:PAIR]),
    ]
    for s in range(SPAN):
        rows_ref[s, 0:PAIR, :] = pieces[s]
        rows_ref[s, PAIR:, :] = jnp.zeros((CHUNK, mine.shape[1]), jnp.bfloat16)


def gram_kernel(core, mine, partner, near, far, packed, rows_ref):
    width = mine.shape[1]
    fill(rows_ref, core, mine, partner, near, far)
    block = {}
    for s in range(SPAN):
        end = min(s + ROUNDS, SPAN)
        others = rows_ref[s:end].reshape((end - s) * LANES, width)
        strip = mm_nt(rows_ref[s, 0:PAIR, :], others)
        for t in range(s, end):
            block[s, t] = strip[:, (t - s) * LANES : (t - s + 1) * LANES]
    lane = iota((PAIR, LANES), 1)
    last = block[LAST]
    for k in range(SLOTS):
        extra = shifted(block[SPREAD[k // 3]], PAIR - CHUNK * (k % 3)) if k < 9 else shifted(last, PAIR)
        whole = jnp.where(lane < PAIR, block[CARRIERS[k]], extra)
        packed[k * PAIR : (k + 1) * PAIR, :] = whole.astype(packed.dtype)
    sides = jnp.where(
        lane[:BLOCK] < LANES // 2, shifted(last[:BLOCK], -CHUNK), shifted(last[BLOCK:], CHUNK)
    )
    packed[SLOTS * PAIR : USED, :] = sides.astype(packed.dtype)
    place = iota((EXTRA, LANES), 0)
    on_diagonal = iota((PAIR, LANES), 0) == lane
    lost = jnp.zeros((EXTRA, LANES), jnp.float32)
    for s in range(SPAN):
        value = block[s, s]
        gone = jnp.where(on_diagonal, value - value.astype(packed.dtype).astype(jnp.float32), 0.0)
        lost = jnp.where(place == s, jnp.sum(gone, axis=0, keepdims=True), lost)
    packed[USED : USED + EXTRA, :] = lost.astype(packed.dtype)
    tail = packed.shape[0] - USED - EXTRA
    if tail:
        packed[USED + EXTRA :, :] = jnp.zeros((tail, LANES), packed.dtype)


def unpacked(packed):
    lane = iota((PAIR, LANES), 1)
    floor = jnp.zeros((CHUNK, LANES), jnp.float32)
    slot = [packed[k * PAIR : (k + 1) * PAIR, :] for k in range(SLOTS)]
    gram = {}
    for k, name in enumerate(CARRIERS):
        gram[name] = jnp.where(lane < PAIR, slot[k], 0.0)
    for m, name in enumerate(SPREAD):
        value = jnp.zeros((PAIR, LANES), jnp.float32)
        for j in range(3):
            here = (lane >= CHUNK * j) & (lane < CHUNK * (j + 1))
            value = jnp.where(here, shifted(slot[3 * m + j], CHUNK * j - PAIR), value)
        gram[name] = value
    rest = packed[SLOTS * PAIR : USED, :]
    sides = jnp.concatenate([shifted(rest, CHUNK), shifted(rest, -CHUNK)], axis=0)
    value = jnp.where(lane < CHUNK, shifted(slot[SLOTS - 1], -PAIR), sides)
    gram[LAST] = jnp.where(lane < PAIR, value, 0.0)
    on_diagonal = iota((PAIR, LANES), 0) == lane
    for s in range(SPAN):
        gram[s, s] += jnp.where(on_diagonal, packed[USED + s : USED + s + 1, :], 0.0)
    return {name: jnp.concatenate([value, floor], axis=0) for name, value in gram.items()}


def product(a, b):
    ah, al = a
    bh, bl = b
    wide = mm(jnp.concatenate([ah, al], axis=0), jnp.concatenate([bh, bl], axis=1))
    return wide[:LANES, :LANES] + (wide[LANES:, :LANES] + wide[:LANES, LANES:])


def turned_rotors(grams):
    shape = (LANES, LANES)
    row, lane = iota(shape, 0), iota(shape, 1)
    inside = (row < PAIR) & (lane < PAIR)
    eye = ((row == lane) & inside).astype(jnp.float32)
    terms = []
    for gram in grams:
        picked = gram * eye
        down = jnp.sum(picked, axis=1, keepdims=True)
        along = jnp.sum(picked, axis=0, keepdims=True)
        gap = along - down
        total = along + down
        bottom = gap * gap + 4.0 * gram * gram + 0.01 * total * total
        theta = gram * gap / jnp.where(inside, bottom, 1.0)
        terms.append(jnp.where(inside, theta, 0.0) * (-1.0 / 64.0))
    first = [halves(e) for e in terms]
    second = [product(a, a) for a in first]
    third = [product(halves(e2), a) for e2, a in zip(second, first)]
    result = []
    for e, e2, e3 in zip(terms, second, third):
        rest = e * (1.0 / 24.0) + e2 * (1.0 / 120.0) + e3 * (1.0 / 720.0)
        result.append(e + e2 * 0.5 + e3 * (1.0 / 6.0) + product(halves(e3), halves(rest)))
    for _ in range(6):
        split = [halves(d) for d in result]
        result = [2.0 * d + product(a, a) for d, a in zip(result, split)]
    return [(d + eye).astype(jnp.bfloat16) for d in result]


def turned_from_left(rows, value):
    high, low = halves(value)
    both = mm(rows, jnp.concatenate([high, low], axis=1))
    return both[:, :LANES] + both[:, LANES:]


def next_grams(gram, turned, count, reach):
    top_lane = iota((LANES, LANES), 1) < BLOCK
    top_half = iota((BLOCK, LANES), 1) < BLOCK
    floor = jnp.zeros((CHUNK, LANES), jnp.float32)
    right = {}
    for t in range(count):
        low = max(0, t - reach)
        stack = []
        for s in range(low, t + 1):
            stack += halves(gram[s, t])
        both = mm_nt(jnp.concatenate(stack, axis=0), turned[t])
        for s in range(low, t + 1):
            at = 2 * (s - low) * LANES
            right[s, t] = both[at : at + LANES] + both[at + LANES : at + 2 * LANES]
    following = {}
    for i in range(count - 1):
        upper, lower = turned[i][0:BLOCK], turned[i + 1][BLOCK:PAIR]
        for j in range(i, min(i + reach, count - 1)):
            top = turned_from_left(upper, jnp.where(top_lane, right[i, j], right[i, j + 1]))
            if i == j:
                bottom = turned_from_left(lower, right[i + 1, j + 1])
                empty = jnp.zeros((LANES - BLOCK, LANES), jnp.float32)
                mirrored = jnp.concatenate([top, empty], axis=0).T[BLOCK:PAIR]
                bottom = jnp.where(top_half, mirrored, bottom)
            else:
                bottom = turned_from_left(lower, jnp.where(top_lane, right[i + 1, j], right[i + 1, j + 1]))
            following[i, j] = jnp.concatenate([top, bottom, floor], axis=0)
    return following


def rounds_kernel(core, packed, mine, partner, near, far, out, sent, rows_ref):
    fill(rows_ref, core, mine, partner, near, far)
    gram = unpacked(packed)
    for step in range(ROUNDS):
        count, reach = SPAN - step, ROUNDS - 1 - step
        turned = turned_rotors([gram[s, s] for s in range(count)])
        if reach == 0:
            break
        gram = next_grams(gram, turned, count, reach)
        for i in range(count):
            old = rows_ref[i]
            if i > 0:
                lower = turned[i][BLOCK:PAIR]
                rows_ref[i - 1, BLOCK:PAIR, :] = mm(lower, old).astype(jnp.bfloat16)
            if i < count - 1:
                upper = turned[i][0:BLOCK]
                rows_ref[i, 0:BLOCK, :] = mm(upper, old).astype(jnp.bfloat16)
    first = core[0] == 0
    ends = [mm(turned[i][0:PAIR], rows_ref[i]).astype(jnp.bfloat16) for i in range(2)]
    out[pl.ds(pl.multiple_of(core[0] * PAIR, PAIR), PAIR), :] = jnp.where(first, ends[0], ends[1])
    sent[...] = jnp.where(first, ends[1], ends[0])


def passed(value, where):
    count = lax.axis_size("col")
    return lax.ppermute(value, "col", [(source, where(source) % count) for source in range(count)])


def on_device(frames, frame_order):
    row_count = lax.axis_size("row")
    width = frames.shape[1] // row_count
    core = lax.axis_index("col") % 2
    arrived = lax.all_to_all(frames, "row", split_axis=1, concat_axis=0, tiled=True)
    order = jnp.where(core == 0, jnp.roll(frame_order, PAIR), frame_order)
    picks = (order[:, None] == iota((1, order.shape[0]), 1)).astype(jnp.bfloat16)
    mine = mm(picks[:PAIR], arrived).astype(jnp.bfloat16)
    other = mm(picks[PAIR:], arrived).astype(jnp.bfloat16)
    partner = passed(other, lambda c: c ^ 1)
    far = passed(mine, lambda c: c - 2 if c % 2 == 0 else c + 2)
    near = passed(jnp.concatenate([mine, partner], axis=0), lambda c: c + 2 if c % 2 == 0 else c - 2)
    held = (mine, partner, near, far)
    chosen = core.astype(jnp.int32).reshape(1)
    share = -(-(USED + EXTRA) // (16 * row_count)) * 16
    limit = pltpu.CompilerParams(vmem_limit_bytes=48 * 1024 * 1024)
    scratch = [pltpu.VMEM((SPAN, LANES, width), jnp.bfloat16)]
    scalar = pl.BlockSpec(memory_space=pltpu.SMEM)
    vector = pl.BlockSpec(memory_space=pltpu.VMEM)
    packed = pl.pallas_call(
        gram_kernel,
        out_shape=jax.ShapeDtypeStruct((share * row_count, LANES), jnp.bfloat16),
        in_specs=[scalar] + [vector] * 4,
        scratch_shapes=scratch,
        compiler_params=limit,
        name="grams",
    )(chosen, *held)
    parts = packed.reshape(row_count, share, LANES)
    parts = lax.all_to_all(parts, "row", split_axis=0, concat_axis=0, tiled=True)
    summed = jnp.sum(parts.astype(jnp.float32), axis=0)
    copies = jnp.broadcast_to(summed[None], (row_count, share, LANES))
    whole = lax.all_to_all(copies, "row", split_axis=0, concat_axis=0, tiled=True)
    half, sent = pl.pallas_call(
        rounds_kernel,
        out_shape=tuple(jax.ShapeDtypeStruct((rows, width), jnp.bfloat16) for rows in (2 * PAIR, PAIR)),
        in_specs=[scalar] + [vector] * 5,
        scratch_shapes=scratch,
        compiler_params=limit,
        name="rounds",
    )(chosen, whole.reshape(row_count * share, LANES), *held)
    got = passed(sent, lambda c: c ^ 1)
    return lax.dynamic_update_slice(half, got, ((1 - core) * PAIR, 0))


def solution(mesh):
    placed = (P(("col", "row"), None), P("col"))
    return jax.shard_map(
        on_device, mesh=mesh, in_specs=placed, out_specs=P("col", "row"), check_vma=False
    )
```

```python
import jax
import jax.numpy as jnp
from jax import lax
from jax.experimental import pallas as pl
from jax.experimental.pallas import tpu as pltpu
from jax.sharding import PartitionSpec as P

BLOCK = 48
PAIR = 2 * BLOCK
LANES = 128
ROUNDS = 4
SPAN = 5
CHUNK = LANES - PAIR

BLOCKS = [(s, t) for s in range(SPAN) for t in range(s + 1, min(s + ROUNDS, SPAN))]
BLOCKS += [(s, s) for s in range(SPAN)]
SLOTS = 10
CARRIERS, SPREAD, LAST = BLOCKS[:SLOTS], BLOCKS[SLOTS : SLOTS + 3], BLOCKS[SLOTS + 3]
USED = SLOTS * PAIR + BLOCK
EXTRA = 16


def iota(shape, dim):
    return lax.broadcasted_iota(jnp.int32, shape, dim)


def mm(a, b):
    return jnp.dot(a, b, preferred_element_type=jnp.float32)


def mm_nt(a, b):
    return lax.dot_general(a, b, (((1,), (1,)), ((), ())), preferred_element_type=jnp.float32)


def halves(value):
    high = value.astype(jnp.bfloat16)
    low = (value - high.astype(jnp.float32)).astype(jnp.bfloat16)
    return high, low


def shifted(value, lanes):
    return pltpu.roll(value, lanes % LANES, 1)


def fill(rows_ref, core, mine, partner, near, far):
    first = core[0] == 0
    pieces = [
        jnp.where(first, near[0:PAIR], far[...]),
        jnp.where(first, near[PAIR:], partner[...]),
        mine[...],
        jnp.where(first, partner[...], near[PAIR:]),
        jnp.where(first, far[...], near[0:PAIR]),
    ]
    for s in range(SPAN):
        rows_ref[s, 0:PAIR, :] = pieces[s]
        rows_ref[s, PAIR:, :] = jnp.zeros((CHUNK, mine.shape[1]), jnp.bfloat16)


def gram_kernel(core, mine, partner, near, far, packed, rows_ref):
    width = mine.shape[1]
    fill(rows_ref, core, mine, partner, near, far)
    block = {}
    for s in range(SPAN):
        end = min(s + ROUNDS, SPAN)
        others = rows_ref[s:end].reshape((end - s) * LANES, width)
        strip = mm_nt(rows_ref[s, 0:PAIR, :], others)
        for t in range(s, end):
            block[s, t] = strip[:, (t - s) * LANES : (t - s + 1) * LANES]
    lane = iota((PAIR, LANES), 1)
    last = block[LAST]
    for k in range(SLOTS):
        extra = shifted(block[SPREAD[k // 3]], PAIR - CHUNK * (k % 3)) if k < 9 else shifted(last, PAIR)
        whole = jnp.where(lane < PAIR, block[CARRIERS[k]], extra)
        packed[k * PAIR : (k + 1) * PAIR, :] = whole.astype(packed.dtype)
    sides = jnp.where(
        lane[:BLOCK] < LANES // 2, shifted(last[:BLOCK], -CHUNK), shifted(last[BLOCK:], CHUNK)
    )
    packed[SLOTS * PAIR : USED, :] = sides.astype(packed.dtype)
    place = iota((EXTRA, LANES), 0)
    on_diagonal = iota((PAIR, LANES), 0) == lane
    lost = jnp.zeros((EXTRA, LANES), jnp.float32)
    for s in range(SPAN):
        value = block[s, s]
        gone = jnp.where(on_diagonal, value - value.astype(packed.dtype).astype(jnp.float32), 0.0)
        lost = jnp.where(place == s, jnp.sum(gone, axis=0, keepdims=True), lost)
    packed[USED : USED + EXTRA, :] = lost.astype(packed.dtype)
    tail = packed.shape[0] - USED - EXTRA
    if tail:
        packed[USED + EXTRA :, :] = jnp.zeros((tail, LANES), packed.dtype)


def unpacked(packed):
    lane = iota((PAIR, LANES), 1)
    floor = jnp.zeros((CHUNK, LANES), jnp.float32)
    slot = [packed[k * PAIR : (k + 1) * PAIR, :] for k in range(SLOTS)]
    gram = {}
    for k, name in enumerate(CARRIERS):
        gram[name] = jnp.where(lane < PAIR, slot[k], 0.0)
    for m, name in enumerate(SPREAD):
        value = jnp.zeros((PAIR, LANES), jnp.float32)
        for j in range(3):
            here = (lane >= CHUNK * j) & (lane < CHUNK * (j + 1))
            value = jnp.where(here, shifted(slot[3 * m + j], CHUNK * j - PAIR), value)
        gram[name] = value
    rest = packed[SLOTS * PAIR : USED, :]
    sides = jnp.concatenate([shifted(rest, CHUNK), shifted(rest, -CHUNK)], axis=0)
    value = jnp.where(lane < CHUNK, shifted(slot[SLOTS - 1], -PAIR), sides)
    gram[LAST] = jnp.where(lane < PAIR, value, 0.0)
    on_diagonal = iota((PAIR, LANES), 0) == lane
    for s in range(SPAN):
        gram[s, s] += jnp.where(on_diagonal, packed[USED + s : USED + s + 1, :], 0.0)
    return {name: jnp.concatenate([value, floor], axis=0) for name, value in gram.items()}


def product(a, b):
    (ah, al), (bh, bl) = a, b
    value = mm(ah[:PAIR], bh) + (mm(al[:PAIR], bh) + mm(ah[:PAIR], bl))
    return jnp.concatenate([value, jnp.zeros((CHUNK, LANES), jnp.float32)], axis=0)


def turned_rotors(grams):
    shape = (LANES, LANES)
    row, lane = iota(shape, 0), iota(shape, 1)
    inside = (row < PAIR) & (lane < PAIR)
    eye = ((row == lane) & inside).astype(jnp.float32)
    terms = []
    for gram in grams:
        picked = gram * eye
        down = jnp.sum(picked, axis=1, keepdims=True)
        along = jnp.sum(picked, axis=0, keepdims=True)
        gap = along - down
        total = along + down
        bottom = gap * gap + 4.0 * gram * gram + 0.01 * total * total
        theta = gram * gap / jnp.where(inside, bottom, 1.0)
        terms.append(jnp.where(inside, theta, 0.0) * (-1.0 / 64.0))
    first = [halves(e) for e in terms]
    second = [product(a, a) for a in first]
    third = [product(halves(e2), a) for e2, a in zip(second, first)]
    result = []
    for e, e2, e3 in zip(terms, second, third):
        rest = e * (1.0 / 24.0) + e2 * (1.0 / 120.0) + e3 * (1.0 / 720.0)
        result.append(e + e2 * 0.5 + e3 * (1.0 / 6.0) + product(halves(e3), halves(rest)))
    for _ in range(6):
        split = [halves(d) for d in result]
        result = [2.0 * d + product(a, a) for d, a in zip(result, split)]
    return [(d + eye).astype(jnp.bfloat16) for d in result]


def turned_from_left(rows, value):
    high, low = halves(value)
    both = mm(rows, jnp.concatenate([high, low], axis=1))
    return both[:, :LANES] + both[:, LANES:]


def next_grams(gram, turned, count, reach):
    top_lane = iota((LANES, LANES), 1) < BLOCK
    top_half = iota((BLOCK, LANES), 1) < BLOCK
    floor = jnp.zeros((CHUNK, LANES), jnp.float32)
    right = {}
    for t in range(count):
        low = max(0, t - reach)
        stack = []
        for s in range(low, t + 1):
            stack += halves(gram[s, t])
        both = mm_nt(jnp.concatenate(stack, axis=0), turned[t])
        for s in range(low, t + 1):
            at = 2 * (s - low) * LANES
            right[s, t] = both[at : at + LANES] + both[at + LANES : at + 2 * LANES]
    following = {}
    for i in range(count - 1):
        upper, lower = turned[i][0:BLOCK], turned[i + 1][BLOCK:PAIR]
        for j in range(i, min(i + reach, count - 1)):
            top = turned_from_left(upper, jnp.where(top_lane, right[i, j], right[i, j + 1]))
            if i == j:
                bottom = turned_from_left(lower, right[i + 1, j + 1])
                empty = jnp.zeros((LANES - BLOCK, LANES), jnp.float32)
                mirrored = jnp.concatenate([top, empty], axis=0).T[BLOCK:PAIR]
                bottom = jnp.where(top_half, mirrored, bottom)
            else:
                bottom = turned_from_left(lower, jnp.where(top_lane, right[i + 1, j], right[i + 1, j + 1]))
            following[i, j] = jnp.concatenate([top, bottom, floor], axis=0)
    return following


def turn(rows, turned, i, into):
    old = rows[i]
    value = mm(turned[i][0:PAIR], old).astype(jnp.bfloat16)
    if i > 0:
        into[i - 1, BLOCK:PAIR, :] = value[BLOCK:]
    if i < into.shape[0]:
        into[i, 0:BLOCK, :] = value[:BLOCK]


def rounds_kernel(core, packed, rows_ref, kept, sent, *later):
    width = kept.shape[1]
    for ref in later:
        for i in range(ref.shape[0]):
            ref[i, PAIR:, :] = jnp.zeros((CHUNK, width), jnp.bfloat16)
    gram = unpacked(packed)
    rows = rows_ref
    for step in range(ROUNDS):
        count, reach = SPAN - step, ROUNDS - 1 - step
        turned = turned_rotors([gram[s, s] for s in range(count)])
        if reach == 0:
            break
        gram = next_grams(gram, turned, count, reach)
        for i in range(count):
            turn(rows, turned, i, later[step])
        rows = later[step]
    first = core[0] == 0
    ends = [mm(turned[i][0:PAIR], rows[i]).astype(jnp.bfloat16) for i in range(2)]
    kept[...] = jnp.where(first, ends[0], ends[1])
    sent[...] = jnp.where(first, ends[1], ends[0])


def passed(value, where):
    count = lax.axis_size("col")
    return lax.ppermute(value, "col", [(source, where(source) % count) for source in range(count)])


def on_device(frames, frame_order):
    row_count = lax.axis_size("row")
    width = frames.shape[1] // row_count
    core = lax.axis_index("col") % 2
    arrived = lax.all_to_all(frames, "row", split_axis=1, concat_axis=0, tiled=True)
    order = jnp.where(core == 0, jnp.roll(frame_order, PAIR), frame_order)
    picks = (order[:, None] == iota((1, order.shape[0]), 1)).astype(jnp.bfloat16)
    mine = mm(picks[:PAIR], arrived).astype(jnp.bfloat16)
    other = mm(picks[PAIR:], arrived).astype(jnp.bfloat16)
    partner = passed(other, lambda c: c ^ 1)
    far = passed(mine, lambda c: c - 2 if c % 2 == 0 else c + 2)
    near = passed(jnp.concatenate([mine, partner], axis=0), lambda c: c + 2 if c % 2 == 0 else c - 2)
    held = (mine, partner, near, far)
    chosen = core.astype(jnp.int32).reshape(1)
    share = -(-(USED + EXTRA) // (16 * row_count)) * 16
    limit = pltpu.CompilerParams(vmem_limit_bytes=48 * 1024 * 1024)
    scalar = pl.BlockSpec(memory_space=pltpu.SMEM)
    vector = pl.BlockSpec(memory_space=pltpu.VMEM)
    packed, rows = pl.pallas_call(
        gram_kernel,
        out_shape=(
            jax.ShapeDtypeStruct((share * row_count, LANES), jnp.bfloat16),
            jax.ShapeDtypeStruct((SPAN, LANES, width), jnp.bfloat16),
        ),
        in_specs=[scalar] + [vector] * 4,
        out_specs=(vector, vector),
        compiler_params=limit,
        name="grams",
    )(chosen, *held)
    parts = packed.reshape(row_count, share, LANES)
    parts = lax.all_to_all(parts, "row", split_axis=0, concat_axis=0, tiled=True)
    summed = jnp.sum(parts.astype(jnp.float32), axis=0)
    copies = jnp.broadcast_to(summed[None], (row_count, share, LANES))
    whole = lax.all_to_all(copies, "row", split_axis=0, concat_axis=0, tiled=True)
    pair = jax.ShapeDtypeStruct((PAIR, width), jnp.bfloat16)
    kept, sent = pl.pallas_call(
        rounds_kernel,
        out_shape=(pair, pair),
        in_specs=[scalar, vector, vector],
        out_specs=(vector, vector),
        scratch_shapes=[pltpu.VMEM((SPAN - 1 - step, LANES, width), jnp.bfloat16) for step in range(ROUNDS - 1)],
        compiler_params=limit,
        name="rounds",
    )(chosen, whole.reshape(row_count * share, LANES), rows)
    got = passed(sent, lambda c: c ^ 1)
    return jnp.concatenate([jnp.where(core == 0, kept, got), jnp.where(core == 0, got, kept)], axis=0)


def solution(mesh):
    placed = (P(("col", "row"), None), P("col"))
    return jax.shard_map(
        on_device, mesh=mesh, in_specs=placed, out_specs=P("col", "row"), check_vma=False
    )
```

```python
import jax
import jax.numpy as jnp
from jax import lax
from jax.experimental import pallas as pl
from jax.experimental.pallas import tpu as pltpu
from jax.sharding import PartitionSpec as P

BLOCK = 48
PAIR = 2 * BLOCK
LANES = 128
ROUNDS = 4
SPAN = 5
CHUNK = LANES - PAIR

BLOCKS = [(s, t) for s in range(SPAN) for t in range(s + 1, min(s + ROUNDS, SPAN))]
BLOCKS += [(s, s) for s in range(SPAN)]
SLOTS = 10
CARRIERS, SPREAD, LAST = BLOCKS[:SLOTS], BLOCKS[SLOTS : SLOTS + 3], BLOCKS[SLOTS + 3]
USED = SLOTS * PAIR + BLOCK
EXTRA = 16


def iota(shape, dim):
    return lax.broadcasted_iota(jnp.int32, shape, dim)


def mm(a, b):
    return jnp.dot(a, b, preferred_element_type=jnp.float32)


def mm_nt(a, b):
    return lax.dot_general(a, b, (((1,), (1,)), ((), ())), preferred_element_type=jnp.float32)


def halves(value):
    high = value.astype(jnp.bfloat16)
    low = (value - high.astype(jnp.float32)).astype(jnp.bfloat16)
    return high, low


def shifted(value, lanes):
    return pltpu.roll(value, lanes % LANES, 1)


def fill(rows_ref, core, mine, partner, near, far):
    first = core[0] == 0
    pieces = [
        jnp.where(first, near[0:PAIR], far[...]),
        jnp.where(first, near[PAIR:], partner[...]),
        mine[...],
        jnp.where(first, partner[...], near[PAIR:]),
        jnp.where(first, far[...], near[0:PAIR]),
    ]
    for s in range(SPAN):
        rows_ref[s, 0:PAIR, :] = pieces[s]
        rows_ref[s, PAIR:, :] = jnp.zeros((CHUNK, mine.shape[1]), jnp.bfloat16)


def gram_kernel(core, mine, partner, near, far, packed, rows_ref):
    width = mine.shape[1]
    fill(rows_ref, core, mine, partner, near, far)
    block = {}
    for s in range(SPAN):
        end = min(s + ROUNDS, SPAN)
        others = rows_ref[s:end].reshape((end - s) * LANES, width)
        strip = mm_nt(rows_ref[s, 0:PAIR, :], others)
        for t in range(s, end):
            block[s, t] = strip[:, (t - s) * LANES : (t - s + 1) * LANES]
    lane = iota((PAIR, LANES), 1)
    last = block[LAST]
    for k in range(SLOTS):
        extra = shifted(block[SPREAD[k // 3]], PAIR - CHUNK * (k % 3)) if k < 9 else shifted(last, PAIR)
        whole = jnp.where(lane < PAIR, block[CARRIERS[k]], extra)
        packed[k * PAIR : (k + 1) * PAIR, :] = whole.astype(packed.dtype)
    sides = jnp.where(
        lane[:BLOCK] < LANES // 2, shifted(last[:BLOCK], -CHUNK), shifted(last[BLOCK:], CHUNK)
    )
    packed[SLOTS * PAIR : USED, :] = sides.astype(packed.dtype)
    place = iota((EXTRA, LANES), 0)
    on_diagonal = iota((PAIR, LANES), 0) == lane
    lost = jnp.zeros((EXTRA, LANES), jnp.float32)
    for s in range(SPAN):
        value = block[s, s]
        gone = jnp.where(on_diagonal, value - value.astype(packed.dtype).astype(jnp.float32), 0.0)
        lost = jnp.where(place == s, jnp.sum(gone, axis=0, keepdims=True), lost)
    packed[USED : USED + EXTRA, :] = lost.astype(packed.dtype)
    tail = packed.shape[0] - USED - EXTRA
    if tail:
        packed[USED + EXTRA :, :] = jnp.zeros((tail, LANES), packed.dtype)


def unpacked(packed):
    lane = iota((PAIR, LANES), 1)
    floor = jnp.zeros((CHUNK, LANES), jnp.float32)
    slot = [packed[k * PAIR : (k + 1) * PAIR, :] for k in range(SLOTS)]
    gram = {}
    for k, name in enumerate(CARRIERS):
        gram[name] = jnp.where(lane < PAIR, slot[k], 0.0)
    for m, name in enumerate(SPREAD):
        value = jnp.zeros((PAIR, LANES), jnp.float32)
        for j in range(3):
            here = (lane >= CHUNK * j) & (lane < CHUNK * (j + 1))
            value = jnp.where(here, shifted(slot[3 * m + j], CHUNK * j - PAIR), value)
        gram[name] = value
    rest = packed[SLOTS * PAIR : USED, :]
    sides = jnp.concatenate([shifted(rest, CHUNK), shifted(rest, -CHUNK)], axis=0)
    value = jnp.where(lane < CHUNK, shifted(slot[SLOTS - 1], -PAIR), sides)
    gram[LAST] = jnp.where(lane < PAIR, value, 0.0)
    on_diagonal = iota((PAIR, LANES), 0) == lane
    for s in range(SPAN):
        gram[s, s] += jnp.where(on_diagonal, packed[USED + s : USED + s + 1, :], 0.0)
    return {name: jnp.concatenate([value, floor], axis=0) for name, value in gram.items()}


def product(a, b):
    (ah, al), (bh, bl) = a, b
    value = mm(ah[:PAIR], bh) + (mm(al[:PAIR], bh) + mm(ah[:PAIR], bl))
    return jnp.concatenate([value, jnp.zeros((CHUNK, LANES), jnp.float32)], axis=0)


def turned_rotors(grams):
    shape = (LANES, LANES)
    row, lane = iota(shape, 0), iota(shape, 1)
    inside = (row < PAIR) & (lane < PAIR)
    eye = ((row == lane) & inside).astype(jnp.float32)
    terms = []
    for gram in grams:
        picked = gram * eye
        down = jnp.sum(picked, axis=1, keepdims=True)
        along = jnp.sum(picked, axis=0, keepdims=True)
        gap = along - down
        total = along + down
        bottom = gap * gap + 4.0 * gram * gram + 0.01 * total * total
        theta = gram * gap / jnp.where(inside, bottom, 1.0)
        terms.append(jnp.where(inside, theta, 0.0) * (-1.0 / 64.0))
    first = [halves(e) for e in terms]
    second = [product(a, a) for a in first]
    third = [product(halves(e2), a) for e2, a in zip(second, first)]
    result = []
    for e, e2, e3 in zip(terms, second, third):
        rest = e * (1.0 / 24.0) + e2 * (1.0 / 120.0) + e3 * (1.0 / 720.0)
        result.append(e + e2 * 0.5 + e3 * (1.0 / 6.0) + product(halves(e3), halves(rest)))
    for _ in range(6):
        split = [halves(d) for d in result]
        result = [2.0 * d + product(a, a) for d, a in zip(result, split)]
    return [(d + eye).astype(jnp.bfloat16) for d in result]


def turned_from_left(rows, value):
    high, low = halves(value)
    both = mm(rows, jnp.concatenate([high, low], axis=1))
    return both[:, :LANES] + both[:, LANES:]


def next_grams(gram, turned, count, reach):
    top_lane = iota((LANES, LANES), 1) < BLOCK
    top_half = iota((BLOCK, LANES), 1) < BLOCK
    floor = jnp.zeros((CHUNK, LANES), jnp.float32)
    right = {}
    for t in range(count):
        low = max(0, t - reach)
        stack = []
        for s in range(low, t + 1):
            stack += halves(gram[s, t])
        both = mm_nt(jnp.concatenate(stack, axis=0), turned[t])
        for s in range(low, t + 1):
            at = 2 * (s - low) * LANES
            right[s, t] = both[at : at + LANES] + both[at + LANES : at + 2 * LANES]
    following = {}
    for i in range(count - 1):
        upper, lower = turned[i][0:BLOCK], turned[i + 1][BLOCK:PAIR]
        for j in range(i, min(i + reach, count - 1)):
            top = turned_from_left(upper, jnp.where(top_lane, right[i, j], right[i, j + 1]))
            if i == j:
                bottom = turned_from_left(lower, right[i + 1, j + 1])
                empty = jnp.zeros((LANES - BLOCK, LANES), jnp.float32)
                mirrored = jnp.concatenate([top, empty], axis=0).T[BLOCK:PAIR]
                bottom = jnp.where(top_half, mirrored, bottom)
            else:
                bottom = turned_from_left(lower, jnp.where(top_lane, right[i + 1, j], right[i + 1, j + 1]))
            following[i, j] = jnp.concatenate([top, bottom, floor], axis=0)
    return following


def turn(rows, turned, i, into):
    old = rows[i]
    value = mm(turned[i][0:PAIR], old).astype(jnp.bfloat16)
    if i > 0:
        into[i - 1, BLOCK:PAIR, :] = value[BLOCK:]
    if i < into.shape[0]:
        into[i, 0:BLOCK, :] = value[:BLOCK]


def rounds_kernel(core, packed, rows_ref, kept, sent, *later):
    width = kept.shape[1]
    for ref in later:
        for i in range(ref.shape[0]):
            ref[i, PAIR:, :] = jnp.zeros((CHUNK, width), jnp.bfloat16)
    gram = unpacked(packed)
    rows = rows_ref
    for step in range(ROUNDS):
        count, reach = SPAN - step, ROUNDS - 1 - step
        turned = turned_rotors([gram[s, s] for s in range(count)])
        if reach == 0:
            break
        gram = next_grams(gram, turned, count, reach)
        for i in range(count):
            turn(rows, turned, i, later[step])
        rows = later[step]
    first = core[0] == 0
    ends = [mm(turned[i][0:PAIR], rows[i]).astype(jnp.bfloat16) for i in range(2)]
    kept[...] = jnp.where(first, ends[0], ends[1])
    sent[...] = jnp.where(first, ends[1], ends[0])


def passed(value, where):
    count = lax.axis_size("col")
    return lax.ppermute(value, "col", [(source, where(source) % count) for source in range(count)])


def on_device(frames, frame_order):
    row_count = lax.axis_size("row")
    width = frames.shape[1] // row_count
    core = lax.axis_index("col") % 2
    deep = width // LANES
    tiles = frames.reshape(-1, row_count, deep, LANES).transpose(1, 0, 2, 3)
    tiles = tiles.reshape(row_count, -1, LANES)
    arrived = lax.all_to_all(tiles, "row", split_axis=0, concat_axis=0, tiled=True)
    arrived = arrived.reshape(frame_order.shape[0], width)
    order = jnp.where(core == 0, jnp.roll(frame_order, PAIR), frame_order)
    picks = (order[:, None] == iota((1, order.shape[0]), 1)).astype(jnp.bfloat16)
    mine = mm(picks[:PAIR], arrived).astype(jnp.bfloat16)
    other = mm(picks[PAIR:], arrived).astype(jnp.bfloat16)
    partner = passed(other, lambda c: c ^ 1)
    far = passed(mine, lambda c: c - 2 if c % 2 == 0 else c + 2)
    near = passed(jnp.concatenate([mine, partner], axis=0), lambda c: c + 2 if c % 2 == 0 else c - 2)
    held = (mine, partner, near, far)
    chosen = core.astype(jnp.int32).reshape(1)
    share = -(-(USED + EXTRA) // (16 * row_count)) * 16
    limit = pltpu.CompilerParams(vmem_limit_bytes=48 * 1024 * 1024)
    scalar = pl.BlockSpec(memory_space=pltpu.SMEM)
    vector = pl.BlockSpec(memory_space=pltpu.VMEM)
    packed, rows = pl.pallas_call(
        gram_kernel,
        out_shape=(
            jax.ShapeDtypeStruct((share * row_count, LANES), jnp.bfloat16),
            jax.ShapeDtypeStruct((SPAN, LANES, width), jnp.bfloat16),
        ),
        in_specs=[scalar] + [vector] * 4,
        out_specs=(vector, vector),
        compiler_params=limit,
        name="grams",
    )(chosen, *held)
    parts = packed.reshape(row_count, share, LANES)
    parts = lax.all_to_all(parts, "row", split_axis=0, concat_axis=0, tiled=True)
    summed = jnp.sum(parts.astype(jnp.float32), axis=0)
    copies = jnp.broadcast_to(summed[None], (row_count, share, LANES))
    whole = lax.all_to_all(copies, "row", split_axis=0, concat_axis=0, tiled=True)
    pair = jax.ShapeDtypeStruct((PAIR, width), jnp.bfloat16)
    kept, sent = pl.pallas_call(
        rounds_kernel,
        out_shape=(pair, pair),
        in_specs=[scalar, vector, vector],
        out_specs=(vector, vector),
        scratch_shapes=[pltpu.VMEM((SPAN - 1 - step, LANES, width), jnp.bfloat16) for step in range(ROUNDS - 1)],
        compiler_params=limit,
        name="rounds",
    )(chosen, whole.reshape(row_count * share, LANES), rows)
    got = passed(sent, lambda c: c ^ 1)
    return jnp.concatenate([jnp.where(core == 0, kept, got), jnp.where(core == 0, got, kept)], axis=0)


def solution(mesh):
    placed = (P(("col", "row"), None), P("col"))
    return jax.shard_map(
        on_device, mesh=mesh, in_specs=placed, out_specs=P("col", "row"), check_vma=False
    )
```

```python
import jax
import jax.numpy as jnp
from jax import lax
from jax.experimental import pallas as pl
from jax.experimental.pallas import tpu as pltpu
from jax.sharding import PartitionSpec as P

BLOCK = 48
PAIR = 2 * BLOCK
LANES = 128
ROUNDS = 4
SPAN = 5
CHUNK = LANES - PAIR

BLOCKS = [(s, t) for s in range(SPAN) for t in range(s + 1, min(s + ROUNDS, SPAN))]
BLOCKS += [(s, s) for s in range(SPAN)]
SLOTS = 10
CARRIERS, SPREAD, LAST = BLOCKS[:SLOTS], BLOCKS[SLOTS : SLOTS + 3], BLOCKS[SLOTS + 3]
USED = SLOTS * PAIR + BLOCK


def iota(shape, dim):
    return lax.broadcasted_iota(jnp.int32, shape, dim)


def mm(a, b):
    return jnp.dot(a, b, preferred_element_type=jnp.float32)


def mm_nt(a, b):
    return lax.dot_general(a, b, (((1,), (1,)), ((), ())), preferred_element_type=jnp.float32)


def halves(value):
    high = value.astype(jnp.bfloat16)
    low = (value - high.astype(jnp.float32)).astype(jnp.bfloat16)
    return high, low


def shifted(value, lanes):
    return pltpu.roll(value, lanes % LANES, 1)


def fill(rows_ref, core, mine, partner, near, far):
    first = core[0] == 0
    pieces = [
        jnp.where(first, near[0:PAIR], far[...]),
        jnp.where(first, near[PAIR:], partner[...]),
        mine[...],
        jnp.where(first, partner[...], near[PAIR:]),
        jnp.where(first, far[...], near[0:PAIR]),
    ]
    for s in range(SPAN):
        rows_ref[s, 0:PAIR, :] = pieces[s]
        rows_ref[s, PAIR:, :] = jnp.zeros((CHUNK, mine.shape[1]), jnp.bfloat16)


def gram_kernel(core, mine, partner, near, far, packed, rows_ref):
    width = mine.shape[1]
    fill(rows_ref, core, mine, partner, near, far)
    block = {}
    for s in range(SPAN):
        end = min(s + ROUNDS, SPAN)
        others = rows_ref[s:end].reshape((end - s) * LANES, width)
        strip = mm_nt(rows_ref[s, 0:PAIR, :], others)
        for t in range(s, end):
            block[s, t] = strip[:, (t - s) * LANES : (t - s + 1) * LANES]
    lane = iota((PAIR, LANES), 1)
    last = block[LAST]
    for k in range(SLOTS):
        extra = shifted(block[SPREAD[k // 3]], PAIR - CHUNK * (k % 3)) if k < 9 else shifted(last, PAIR)
        whole = jnp.where(lane < PAIR, block[CARRIERS[k]], extra)
        packed[k * PAIR : (k + 1) * PAIR, :] = whole
    sides = jnp.where(
        lane[:BLOCK] < LANES // 2, shifted(last[:BLOCK], -CHUNK), shifted(last[BLOCK:], CHUNK)
    )
    packed[SLOTS * PAIR : USED, :] = sides
    tail = packed.shape[0] - USED
    if tail:
        packed[USED:, :] = jnp.zeros((tail, LANES), jnp.float32)


def unpacked(packed):
    lane = iota((PAIR, LANES), 1)
    floor = jnp.zeros((CHUNK, LANES), jnp.float32)
    slot = [packed[k * PAIR : (k + 1) * PAIR, :] for k in range(SLOTS)]
    gram = {}
    for k, name in enumerate(CARRIERS):
        gram[name] = jnp.where(lane < PAIR, slot[k], 0.0)
    for m, name in enumerate(SPREAD):
        value = jnp.zeros((PAIR, LANES), jnp.float32)
        for j in range(3):
            here = (lane >= CHUNK * j) & (lane < CHUNK * (j + 1))
            value = jnp.where(here, shifted(slot[3 * m + j], CHUNK * j - PAIR), value)
        gram[name] = value
    rest = packed[SLOTS * PAIR : USED, :]
    sides = jnp.concatenate([shifted(rest, CHUNK), shifted(rest, -CHUNK)], axis=0)
    value = jnp.where(lane < CHUNK, shifted(slot[SLOTS - 1], -PAIR), sides)
    gram[LAST] = jnp.where(lane < PAIR, value, 0.0)
    return {name: jnp.concatenate([value, floor], axis=0) for name, value in gram.items()}


def product(a, b):
    (ah, al), (bh, bl) = a, b
    value = mm(ah[:PAIR], bh) + (mm(al[:PAIR], bh) + mm(ah[:PAIR], bl))
    return jnp.concatenate([value, jnp.zeros((CHUNK, LANES), jnp.float32)], axis=0)


def turned_rotors(grams):
    shape = (LANES, LANES)
    row, lane = iota(shape, 0), iota(shape, 1)
    inside = (row < PAIR) & (lane < PAIR)
    eye = ((row == lane) & inside).astype(jnp.float32)
    terms = []
    for gram in grams:
        picked = gram * eye
        down = jnp.sum(picked, axis=1, keepdims=True)
        along = jnp.sum(picked, axis=0, keepdims=True)
        gap = along - down
        total = along + down
        bottom = gap * gap + 4.0 * gram * gram + 0.01 * total * total
        theta = gram * gap / jnp.where(inside, bottom, 1.0)
        terms.append(jnp.where(inside, theta, 0.0) * (-1.0 / 64.0))
    first = [halves(e) for e in terms]
    second = [product(a, a) for a in first]
    third = [product(halves(e2), a) for e2, a in zip(second, first)]
    result = []
    for e, e2, e3 in zip(terms, second, third):
        rest = e * (1.0 / 24.0) + e2 * (1.0 / 120.0) + e3 * (1.0 / 720.0)
        result.append(e + e2 * 0.5 + e3 * (1.0 / 6.0) + product(halves(e3), halves(rest)))
    for _ in range(6):
        split = [halves(d) for d in result]
        result = [2.0 * d + product(a, a) for d, a in zip(result, split)]
    return [(d + eye).astype(jnp.bfloat16) for d in result]


def turned_from_left(rows, value):
    high, low = halves(value)
    both = mm(rows, jnp.concatenate([high, low], axis=1))
    return both[:, :LANES] + both[:, LANES:]


def next_grams(gram, turned, count, reach):
    top_lane = iota((LANES, LANES), 1) < BLOCK
    top_half = iota((BLOCK, LANES), 1) < BLOCK
    floor = jnp.zeros((CHUNK, LANES), jnp.float32)
    right = {}
    for t in range(count):
        low = max(0, t - reach)
        stack = []
        for s in range(low, t + 1):
            stack += halves(gram[s, t])
        both = mm_nt(jnp.concatenate(stack, axis=0), turned[t])
        for s in range(low, t + 1):
            at = 2 * (s - low) * LANES
            right[s, t] = both[at : at + LANES] + both[at + LANES : at + 2 * LANES]
    following = {}
    for i in range(count - 1):
        upper, lower = turned[i][0:BLOCK], turned[i + 1][BLOCK:PAIR]
        for j in range(i, min(i + reach, count - 1)):
            top = turned_from_left(upper, jnp.where(top_lane, right[i, j], right[i, j + 1]))
            if i == j:
                bottom = turned_from_left(lower, right[i + 1, j + 1])
                empty = jnp.zeros((LANES - BLOCK, LANES), jnp.float32)
                mirrored = jnp.concatenate([top, empty], axis=0).T[BLOCK:PAIR]
                bottom = jnp.where(top_half, mirrored, bottom)
            else:
                bottom = turned_from_left(lower, jnp.where(top_lane, right[i + 1, j], right[i + 1, j + 1]))
            following[i, j] = jnp.concatenate([top, bottom, floor], axis=0)
    return following


def turn(rows, turned, i, into):
    old = rows[i]
    value = mm(turned[i][0:PAIR], old).astype(jnp.bfloat16)
    if i > 0:
        into[i - 1, BLOCK:PAIR, :] = value[BLOCK:]
    if i < into.shape[0]:
        into[i, 0:BLOCK, :] = value[:BLOCK]


def rounds_kernel(core, packed, rows_ref, kept, sent, *later):
    width = kept.shape[1]
    for ref in later:
        for i in range(ref.shape[0]):
            ref[i, PAIR:, :] = jnp.zeros((CHUNK, width), jnp.bfloat16)
    gram = unpacked(packed)
    rows = rows_ref
    for step in range(ROUNDS):
        count, reach = SPAN - step, ROUNDS - 1 - step
        turned = turned_rotors([gram[s, s] for s in range(count)])
        if reach == 0:
            break
        gram = next_grams(gram, turned, count, reach)
        for i in range(count):
            turn(rows, turned, i, later[step])
        rows = later[step]
    first = core[0] == 0
    ends = [mm(turned[i][0:PAIR], rows[i]).astype(jnp.bfloat16) for i in range(2)]
    kept[...] = jnp.where(first, ends[0], ends[1])
    sent[...] = jnp.where(first, ends[1], ends[0])


def passed(value, where):
    count = lax.axis_size("col")
    return lax.ppermute(value, "col", [(source, where(source) % count) for source in range(count)])


def on_device(frames, frame_order):
    row_count = lax.axis_size("row")
    width = frames.shape[1] // row_count
    core = lax.axis_index("col") % 2
    deep = width // LANES
    tiles = frames.reshape(-1, row_count, deep, LANES).transpose(1, 0, 2, 3)
    tiles = tiles.reshape(row_count, -1, LANES)
    arrived = lax.all_to_all(tiles, "row", split_axis=0, concat_axis=0, tiled=True)
    arrived = arrived.reshape(frame_order.shape[0], width)
    order = jnp.where(core == 0, jnp.roll(frame_order, PAIR), frame_order)
    picks = (order[:, None] == iota((1, order.shape[0]), 1)).astype(jnp.bfloat16)
    mine = mm(picks[:PAIR], arrived).astype(jnp.bfloat16)
    other = mm(picks[PAIR:], arrived).astype(jnp.bfloat16)
    partner = passed(other, lambda c: c ^ 1)
    far = passed(mine, lambda c: c - 2 if c % 2 == 0 else c + 2)
    near = passed(jnp.concatenate([mine, partner], axis=0), lambda c: c + 2 if c % 2 == 0 else c - 2)
    held = (mine, partner, near, far)
    chosen = core.astype(jnp.int32).reshape(1)
    share = -(-USED // (8 * row_count)) * 8
    limit = pltpu.CompilerParams(vmem_limit_bytes=48 * 1024 * 1024)
    scalar = pl.BlockSpec(memory_space=pltpu.SMEM)
    vector = pl.BlockSpec(memory_space=pltpu.VMEM)
    packed, rows = pl.pallas_call(
        gram_kernel,
        out_shape=(
            jax.ShapeDtypeStruct((share * row_count, LANES), jnp.float32),
            jax.ShapeDtypeStruct((SPAN, LANES, width), jnp.bfloat16),
        ),
        in_specs=[scalar] + [vector] * 4,
        out_specs=(vector, vector),
        compiler_params=limit,
        name="grams",
    )(chosen, *held)
    parts = packed.reshape(row_count, share, LANES)
    parts = lax.all_to_all(parts, "row", split_axis=0, concat_axis=0, tiled=True)
    summed = jnp.sum(parts, axis=0)
    copies = jnp.broadcast_to(summed[None], (row_count, share, LANES))
    whole = lax.all_to_all(copies, "row", split_axis=0, concat_axis=0, tiled=True)
    pair = jax.ShapeDtypeStruct((PAIR, width), jnp.bfloat16)
    kept, sent = pl.pallas_call(
        rounds_kernel,
        out_shape=(pair, pair),
        in_specs=[scalar, vector, vector],
        out_specs=(vector, vector),
        scratch_shapes=[pltpu.VMEM((SPAN - 1 - step, LANES, width), jnp.bfloat16) for step in range(ROUNDS - 1)],
        compiler_params=limit,
        name="rounds",
    )(chosen, whole.reshape(row_count * share, LANES), rows)
    got = passed(sent, lambda c: c ^ 1)
    return jnp.concatenate([jnp.where(core == 0, kept, got), jnp.where(core == 0, got, kept)], axis=0)


def solution(mesh):
    placed = (P(("col", "row"), None), P("col"))
    return jax.shard_map(
        on_device, mesh=mesh, in_specs=placed, out_specs=P("col", "row"), check_vma=False
    )
```

```python
import jax
import jax.numpy as jnp
from jax import lax
from jax.experimental import pallas as pl
from jax.experimental.pallas import tpu as pltpu
from jax.sharding import PartitionSpec as P

BLOCK = 48
PAIR = 2 * BLOCK
LANES = 128
ROUNDS = 4
SPAN = 5
CHUNK = LANES - PAIR

CROSS = [(s, t) for s in range(SPAN) for t in range(s + 1, min(s + ROUNDS, SPAN))]
LEFT, RIGHT = CROSS[:7], [(s, s) for s in range(SPAN)] + CROSS[7:]
HALF = LANES // 2
STEP = PAIR + BLOCK
USED = len(LEFT) * STEP
GROUP = 16


def iota(shape, dim):
    return lax.broadcasted_iota(jnp.int32, shape, dim)


def mm(a, b):
    return jnp.dot(a, b, preferred_element_type=jnp.float32)


def mm_nt(a, b):
    return lax.dot_general(a, b, (((1,), (1,)), ((), ())), preferred_element_type=jnp.float32)


def halves(value):
    high = value.astype(jnp.bfloat16)
    low = (value - high.astype(jnp.float32)).astype(jnp.bfloat16)
    return high, low


def shifted(value, lanes):
    return pltpu.roll(value, lanes % LANES, 1)


def fill(rows_ref, core, mine, partner, near, far):
    first = core[0] == 0
    pieces = [
        jnp.where(first, near[0:PAIR], far[...]),
        jnp.where(first, near[PAIR:], partner[...]),
        mine[...],
        jnp.where(first, partner[...], near[PAIR:]),
        jnp.where(first, far[...], near[0:PAIR]),
    ]
    for s in range(SPAN):
        rows_ref[s, 0:PAIR, :] = pieces[s]
        rows_ref[s, PAIR:, :] = jnp.zeros((CHUNK, mine.shape[1]), jnp.bfloat16)


def gram_kernel(core, mine, partner, near, far, packed, rows_ref):
    width = mine.shape[1]
    fill(rows_ref, core, mine, partner, near, far)
    block = {}
    for s in range(SPAN):
        end = min(s + ROUNDS, SPAN)
        others = rows_ref[s:end].reshape((end - s) * LANES, width)
        strip = mm_nt(rows_ref[s, 0:PAIR, :], others)
        for t in range(s, end):
            block[s, t] = strip[:, (t - s) * LANES : (t - s + 1) * LANES]
    lane = iota((PAIR, LANES), 1)
    short = lane[:BLOCK]
    flat = []
    for one, two in zip(LEFT, RIGHT):
        one, two = block[one], block[two]
        flat.append(jnp.where(lane < HALF, one, shifted(two, HALF)))
        first = jnp.where(short < CHUNK, shifted(one[:BLOCK], -HALF), shifted(one[BLOCK:], -CHUNK))
        second = jnp.where(short < PAIR, two[:BLOCK], shifted(two[BLOCK:], CHUNK))
        flat.append(jnp.where(short < HALF, first, second))
    groups = packed.shape[0] // (3 * GROUP // 2)
    flat.append(jnp.zeros((groups * GROUP - USED, LANES), jnp.float32))
    flat = jnp.concatenate(flat, axis=0)
    left = iota((GROUP // 2, LANES), 1) < HALF
    for pair in range(groups // 2):
        rows = []
        for at in (2 * pair * GROUP, (2 * pair + 1) * GROUP):
            value = flat[at : at + GROUP]
            lost = value - value.astype(jnp.bfloat16).astype(jnp.float32)
            lost = jnp.where(left, shifted(lost[: GROUP // 2], HALF), lost[GROUP // 2 :])
            rows += [value, lost]
        packed[3 * GROUP * pair : 3 * GROUP * (pair + 1), :] = jnp.concatenate(rows, axis=0).astype(jnp.bfloat16)


def restored(sums):
    sums = sums.reshape(-1, 3 * GROUP // 2, LANES)
    high, lost = sums[:, :GROUP], sums[:, GROUP:]
    lost = jnp.concatenate([lost[:, :, :HALF], lost[:, :, HALF:]], axis=1)
    return (high + jnp.pad(lost, ((0, 0), (0, 0), (HALF, 0)))).reshape(-1, LANES)


def unpacked(packed):
    lane = iota((PAIR, LANES), 1)
    floor = jnp.zeros((CHUNK, LANES), jnp.float32)
    gram = {}
    for k, (one, two) in enumerate(zip(LEFT, RIGHT)):
        main = packed[k * STEP : k * STEP + PAIR, :]
        rest = packed[k * STEP + PAIR : (k + 1) * STEP, :]
        sides = jnp.concatenate([shifted(rest, HALF), shifted(rest, CHUNK)], axis=0)
        gram[one] = jnp.where(lane < HALF, main, jnp.where(lane < PAIR, sides, 0.0))
        sides = jnp.concatenate([rest, shifted(rest, -CHUNK)], axis=0)
        gram[two] = jnp.where(lane < HALF, shifted(main, HALF), jnp.where(lane < PAIR, sides, 0.0))
    return {name: jnp.concatenate([value, floor], axis=0) for name, value in gram.items()}


def product(a, b):
    (ah, al), (bh, bl) = a, b
    value = mm(ah[:PAIR], bh) + (mm(al[:PAIR], bh) + mm(ah[:PAIR], bl))
    return jnp.concatenate([value, jnp.zeros((CHUNK, LANES), jnp.float32)], axis=0)


def turned_rotors(grams):
    shape = (LANES, LANES)
    row, lane = iota(shape, 0), iota(shape, 1)
    inside = (row < PAIR) & (lane < PAIR)
    eye = ((row == lane) & inside).astype(jnp.float32)
    terms = []
    for gram in grams:
        picked = gram * eye
        down = jnp.sum(picked, axis=1, keepdims=True)
        along = jnp.sum(picked, axis=0, keepdims=True)
        gap = along - down
        total = along + down
        bottom = gap * gap + 4.0 * gram * gram + 0.01 * total * total
        theta = gram * gap / jnp.where(inside, bottom, 1.0)
        terms.append(jnp.where(inside, theta, 0.0) * (-1.0 / 64.0))
    first = [halves(e) for e in terms]
    second = [product(a, a) for a in first]
    third = [product(halves(e2), a) for e2, a in zip(second, first)]
    result = []
    for e, e2, e3 in zip(terms, second, third):
        rest = e * (1.0 / 24.0) + e2 * (1.0 / 120.0) + e3 * (1.0 / 720.0)
        result.append(e + e2 * 0.5 + e3 * (1.0 / 6.0) + product(halves(e3), halves(rest)))
    for _ in range(6):
        split = [halves(d) for d in result]
        result = [2.0 * d + product(a, a) for d, a in zip(result, split)]
    return [(d + eye).astype(jnp.bfloat16) for d in result]


def turned_from_left(rows, value):
    high, low = halves(value)
    both = mm(rows, jnp.concatenate([high, low], axis=1))
    return both[:, :LANES] + both[:, LANES:]


def next_grams(gram, turned, count, reach):
    top_lane = iota((LANES, LANES), 1) < BLOCK
    top_half = iota((BLOCK, LANES), 1) < BLOCK
    floor = jnp.zeros((CHUNK, LANES), jnp.float32)
    right = {}
    for t in range(count):
        low = max(0, t - reach)
        stack = []
        for s in range(low, t + 1):
            stack += halves(gram[s, t])
        both = mm_nt(jnp.concatenate(stack, axis=0), turned[t])
        for s in range(low, t + 1):
            at = 2 * (s - low) * LANES
            right[s, t] = both[at : at + LANES] + both[at + LANES : at + 2 * LANES]
    following = {}
    for i in range(count - 1):
        upper, lower = turned[i][0:BLOCK], turned[i + 1][BLOCK:PAIR]
        for j in range(i, min(i + reach, count - 1)):
            top = turned_from_left(upper, jnp.where(top_lane, right[i, j], right[i, j + 1]))
            if i == j:
                bottom = turned_from_left(lower, right[i + 1, j + 1])
                empty = jnp.zeros((LANES - BLOCK, LANES), jnp.float32)
                mirrored = jnp.concatenate([top, empty], axis=0).T[BLOCK:PAIR]
                bottom = jnp.where(top_half, mirrored, bottom)
            else:
                bottom = turned_from_left(lower, jnp.where(top_lane, right[i + 1, j], right[i + 1, j + 1]))
            following[i, j] = jnp.concatenate([top, bottom, floor], axis=0)
    return following


def turn(rows, turned, i, into):
    old = rows[i]
    value = mm(turned[i][0:PAIR], old).astype(jnp.bfloat16)
    if i > 0:
        into[i - 1, BLOCK:PAIR, :] = value[BLOCK:]
    if i < into.shape[0]:
        into[i, 0:BLOCK, :] = value[:BLOCK]


def rounds_kernel(core, packed, rows_ref, kept, sent, *later):
    width = kept.shape[1]
    for ref in later:
        for i in range(ref.shape[0]):
            ref[i, PAIR:, :] = jnp.zeros((CHUNK, width), jnp.bfloat16)
    gram = unpacked(packed)
    rows = rows_ref
    for step in range(ROUNDS):
        count, reach = SPAN - step, ROUNDS - 1 - step
        turned = turned_rotors([gram[s, s] for s in range(count)])
        if reach == 0:
            break
        gram = next_grams(gram, turned, count, reach)
        for i in range(count):
            turn(rows, turned, i, later[step])
        rows = later[step]
    first = core[0] == 0
    ends = [mm(turned[i][0:PAIR], rows[i]).astype(jnp.bfloat16) for i in range(2)]
    kept[...] = jnp.where(first, ends[0], ends[1])
    sent[...] = jnp.where(first, ends[1], ends[0])


def passed(value, where):
    count = lax.axis_size("col")
    return lax.ppermute(value, "col", [(source, where(source) % count) for source in range(count)])


def on_device(frames, frame_order):
    row_count = lax.axis_size("row")
    width = frames.shape[1] // row_count
    core = lax.axis_index("col") % 2
    deep = width // LANES
    tiles = frames.reshape(-1, row_count, deep, LANES).transpose(1, 0, 2, 3)
    tiles = tiles.reshape(row_count, -1, LANES)
    arrived = lax.all_to_all(tiles, "row", split_axis=0, concat_axis=0, tiled=True)
    arrived = arrived.reshape(frame_order.shape[0], width)
    order = jnp.where(core == 0, jnp.roll(frame_order, PAIR), frame_order)
    picks = (order[:, None] == iota((1, order.shape[0]), 1)).astype(jnp.bfloat16)
    mine = mm(picks[:PAIR], arrived).astype(jnp.bfloat16)
    other = mm(picks[PAIR:], arrived).astype(jnp.bfloat16)
    partner = passed(other, lambda c: c ^ 1)
    far = passed(mine, lambda c: c - 2 if c % 2 == 0 else c + 2)
    near = passed(jnp.concatenate([mine, partner], axis=0), lambda c: c + 2 if c % 2 == 0 else c - 2)
    held = (mine, partner, near, far)
    chosen = core.astype(jnp.int32).reshape(1)
    share = -(-USED // (GROUP * row_count)) * GROUP
    limit = pltpu.CompilerParams(vmem_limit_bytes=48 * 1024 * 1024)
    scalar = pl.BlockSpec(memory_space=pltpu.SMEM)
    vector = pl.BlockSpec(memory_space=pltpu.VMEM)
    packed, rows = pl.pallas_call(
        gram_kernel,
        out_shape=(
            jax.ShapeDtypeStruct((share * 3 // 2 * row_count, LANES), jnp.bfloat16),
            jax.ShapeDtypeStruct((SPAN, LANES, width), jnp.bfloat16),
        ),
        in_specs=[scalar] + [vector] * 4,
        out_specs=(vector, vector),
        compiler_params=limit,
        name="grams",
    )(chosen, *held)
    parts = packed.reshape(row_count, share * 3 // 2, LANES)
    parts = lax.all_to_all(parts, "row", split_axis=0, concat_axis=0, tiled=True)
    summed = restored(jnp.sum(parts.astype(jnp.float32), axis=0))
    copies = jnp.broadcast_to(summed[None], (row_count, share, LANES))
    whole = lax.all_to_all(copies, "row", split_axis=0, concat_axis=0, tiled=True)
    pair = jax.ShapeDtypeStruct((PAIR, width), jnp.bfloat16)
    kept, sent = pl.pallas_call(
        rounds_kernel,
        out_shape=(pair, pair),
        in_specs=[scalar, vector, vector],
        out_specs=(vector, vector),
        scratch_shapes=[pltpu.VMEM((SPAN - 1 - step, LANES, width), jnp.bfloat16) for step in range(ROUNDS - 1)],
        compiler_params=limit,
        name="rounds",
    )(chosen, whole.reshape(row_count * share, LANES), rows)
    got = passed(sent, lambda c: c ^ 1)
    return jnp.concatenate([jnp.where(core == 0, kept, got), jnp.where(core == 0, got, kept)], axis=0)


def solution(mesh):
    placed = (P(("col", "row"), None), P("col"))
    return jax.shard_map(
        on_device, mesh=mesh, in_specs=placed, out_specs=P("col", "row"), check_vma=False
    )
```

```python
import jax
import jax.numpy as jnp
from jax import lax
from jax.experimental import pallas as pl
from jax.experimental.pallas import tpu as pltpu
from jax.sharding import PartitionSpec as P

BLOCK = 48
PAIR = 2 * BLOCK
LANES = 128
ROUNDS = 4
SPAN = 5
CHUNK = LANES - PAIR

CROSS = [(s, t) for s in range(SPAN) for t in range(s + 1, min(s + ROUNDS, SPAN))]
LEFT, RIGHT = CROSS[:7], [(s, s) for s in range(SPAN)] + CROSS[7:]
HALF = LANES // 2
STEP = PAIR + BLOCK
USED = len(LEFT) * STEP
GROUP = 16


def iota(shape, dim):
    return lax.broadcasted_iota(jnp.int32, shape, dim)


def mm(a, b):
    return jnp.dot(a, b, preferred_element_type=jnp.float32)


def mm_nt(a, b):
    return lax.dot_general(a, b, (((1,), (1,)), ((), ())), preferred_element_type=jnp.float32)


def halves(value):
    high = value.astype(jnp.bfloat16)
    low = (value - high.astype(jnp.float32)).astype(jnp.bfloat16)
    return high, low


def shifted(value, lanes):
    return pltpu.roll(value, lanes % LANES, 1)


def fill(rows_ref, core, mine, partner, near, far):
    first = core[0] == 0
    pieces = [
        jnp.where(first, near[0:PAIR], far[...]),
        jnp.where(first, near[PAIR:], partner[...]),
        mine[...],
        jnp.where(first, partner[...], near[PAIR:]),
        jnp.where(first, far[...], near[0:PAIR]),
    ]
    for s in range(SPAN):
        rows_ref[s, 0:PAIR, :] = pieces[s]
        rows_ref[s, PAIR:, :] = jnp.zeros((CHUNK, mine.shape[1]), jnp.bfloat16)


def gram_kernel(core, mine, partner, near, far, packed, rows_ref):
    width = mine.shape[1]
    fill(rows_ref, core, mine, partner, near, far)
    block = {}
    for s in range(SPAN):
        end = min(s + ROUNDS, SPAN)
        others = rows_ref[s:end].reshape((end - s) * LANES, width)
        strip = mm_nt(rows_ref[s, 0:PAIR, :], others)
        for t in range(s, end):
            block[s, t] = strip[:, (t - s) * LANES : (t - s + 1) * LANES]
    lane = iota((PAIR, LANES), 1)
    short = lane[:BLOCK]
    flat = []
    for one, two in zip(LEFT, RIGHT):
        one, two = block[one], block[two]
        flat.append(jnp.where(lane < HALF, one, shifted(two, HALF)))
        first = jnp.where(short < CHUNK, shifted(one[:BLOCK], -HALF), shifted(one[BLOCK:], -CHUNK))
        second = jnp.where(short < PAIR, two[:BLOCK], shifted(two[BLOCK:], CHUNK))
        flat.append(jnp.where(short < HALF, first, second))
    groups = packed.shape[0] // (3 * GROUP // 2)
    flat.append(jnp.zeros((groups * GROUP - USED, LANES), jnp.float32))
    flat = jnp.concatenate(flat, axis=0)
    left = iota((GROUP // 2, LANES), 1) < HALF
    for pair in range(groups // 2):
        rows = []
        for at in (2 * pair * GROUP, (2 * pair + 1) * GROUP):
            value = flat[at : at + GROUP]
            lost = value - value.astype(jnp.bfloat16).astype(jnp.float32)
            lost = jnp.where(left, shifted(lost[: GROUP // 2], HALF), lost[GROUP // 2 :])
            rows += [value, lost]
        packed[3 * GROUP * pair : 3 * GROUP * (pair + 1), :] = jnp.concatenate(rows, axis=0).astype(jnp.bfloat16)


def restored(sums):
    sums = sums.reshape(-1, 3 * GROUP // 2, LANES)
    high, lost = sums[:, :GROUP], sums[:, GROUP:]
    lost = jnp.concatenate([lost[:, :, :HALF], lost[:, :, HALF:]], axis=1)
    return (high + jnp.pad(lost, ((0, 0), (0, 0), (HALF, 0)))).reshape(-1, LANES)


def unpacked(packed):
    lane = iota((PAIR, LANES), 1)
    floor = jnp.zeros((CHUNK, LANES), jnp.float32)
    gram = {}
    for k, (one, two) in enumerate(zip(LEFT, RIGHT)):
        main = packed[k * STEP : k * STEP + PAIR, :]
        rest = packed[k * STEP + PAIR : (k + 1) * STEP, :]
        sides = jnp.concatenate([shifted(rest, HALF), shifted(rest, CHUNK)], axis=0)
        gram[one] = jnp.where(lane < HALF, main, jnp.where(lane < PAIR, sides, 0.0))
        sides = jnp.concatenate([rest, shifted(rest, -CHUNK)], axis=0)
        gram[two] = jnp.where(lane < HALF, shifted(main, HALF), jnp.where(lane < PAIR, sides, 0.0))
    return {name: jnp.concatenate([value, floor], axis=0) for name, value in gram.items()}


def product(a, b):
    (ah, al), (bh, bl) = a, b
    value = mm(ah[:PAIR], bh) + (mm(al[:PAIR], bh) + mm(ah[:PAIR], bl))
    return jnp.concatenate([value, jnp.zeros((CHUNK, LANES), jnp.float32)], axis=0)


def turned_rotors(grams):
    shape = (LANES, LANES)
    row, lane = iota(shape, 0), iota(shape, 1)
    inside = (row < PAIR) & (lane < PAIR)
    eye = ((row == lane) & inside).astype(jnp.float32)
    terms = []
    for gram in grams:
        picked = gram * eye
        down = jnp.sum(picked, axis=1, keepdims=True)
        along = jnp.sum(picked, axis=0, keepdims=True)
        gap = along - down
        total = along + down
        bottom = gap * gap + 4.0 * gram * gram + 0.01 * total * total
        theta = gram * gap / jnp.where(inside, bottom, 1.0)
        terms.append(jnp.where(inside, theta, 0.0) * (-1.0 / 64.0))
    first = [halves(e) for e in terms]
    second = [product(a, a) for a in first]
    third = [product(halves(e2), a) for e2, a in zip(second, first)]
    result = []
    for e, e2, e3 in zip(terms, second, third):
        rest = e * (1.0 / 24.0) + e2 * (1.0 / 120.0) + e3 * (1.0 / 720.0)
        result.append(e + e2 * 0.5 + e3 * (1.0 / 6.0) + product(halves(e3), halves(rest)))
    for _ in range(6):
        split = [halves(d) for d in result]
        result = [2.0 * d + product(a, a) for d, a in zip(result, split)]
    return [(d + eye).astype(jnp.bfloat16) for d in result]


def turned_from_left(rows, value):
    high, low = halves(value)
    both = mm(rows, jnp.concatenate([high, low], axis=1))
    return both[:, :LANES] + both[:, LANES:]


def next_grams(gram, turned, count, reach):
    top_lane = iota((LANES, LANES), 1) < BLOCK
    floor = jnp.zeros((CHUNK, LANES), jnp.float32)
    right = {}
    for t in range(count):
        low = max(0, t - reach)
        blocks = [gram[s, t] for s in range(low, t + 1)]
        if t + 1 < count:
            blocks.append(gram[t, t + 1].T)
        stack = []
        for block in blocks:
            stack += halves(block)
        both = mm_nt(jnp.concatenate(stack, axis=0), turned[t])
        for at in range(len(blocks)):
            high = both[2 * at * LANES : (2 * at + 1) * LANES]
            right[low + at, t] = high + both[(2 * at + 1) * LANES : (2 * at + 2) * LANES]
    following = {}
    for i in range(count - 1):
        upper, lower = turned[i][0:BLOCK], turned[i + 1][BLOCK:PAIR]
        for j in range(i, min(i + reach, count - 1)):
            top = turned_from_left(upper, jnp.where(top_lane, right[i, j], right[i, j + 1]))
            bottom = turned_from_left(lower, jnp.where(top_lane, right[i + 1, j], right[i + 1, j + 1]))
            following[i, j] = jnp.concatenate([top, bottom, floor], axis=0)
    return following


def turn(rows, turned, i, into):
    old = rows[i]
    value = mm(turned[i][0:PAIR], old).astype(jnp.bfloat16)
    if i > 0:
        into[i - 1, BLOCK:PAIR, :] = value[BLOCK:]
    if i < into.shape[0]:
        into[i, 0:BLOCK, :] = value[:BLOCK]


def rounds_kernel(core, packed, rows_ref, kept, sent, *later):
    width = kept.shape[1]
    for ref in later:
        for i in range(ref.shape[0]):
            ref[i, PAIR:, :] = jnp.zeros((CHUNK, width), jnp.bfloat16)
    gram = unpacked(packed)
    rows = rows_ref
    for step in range(ROUNDS):
        count, reach = SPAN - step, ROUNDS - 1 - step
        turned = turned_rotors([gram[s, s] for s in range(count)])
        if reach == 0:
            break
        gram = next_grams(gram, turned, count, reach)
        for i in range(count):
            turn(rows, turned, i, later[step])
        rows = later[step]
    first = core[0] == 0
    ends = [mm(turned[i][0:PAIR], rows[i]).astype(jnp.bfloat16) for i in range(2)]
    kept[...] = jnp.where(first, ends[0], ends[1])
    sent[...] = jnp.where(first, ends[1], ends[0])


def passed(value, where):
    count = lax.axis_size("col")
    return lax.ppermute(value, "col", [(source, where(source) % count) for source in range(count)])


def on_device(frames, frame_order):
    row_count = lax.axis_size("row")
    width = frames.shape[1] // row_count
    core = lax.axis_index("col") % 2
    deep = width // LANES
    tiles = frames.reshape(-1, row_count, deep, LANES).transpose(1, 0, 2, 3)
    tiles = tiles.reshape(row_count, -1, LANES)
    arrived = lax.all_to_all(tiles, "row", split_axis=0, concat_axis=0, tiled=True)
    arrived = arrived.reshape(frame_order.shape[0], width)
    order = jnp.where(core == 0, jnp.roll(frame_order, PAIR), frame_order)
    picks = (order[:, None] == iota((1, order.shape[0]), 1)).astype(jnp.bfloat16)
    mine = mm(picks[:PAIR], arrived).astype(jnp.bfloat16)
    other = mm(picks[PAIR:], arrived).astype(jnp.bfloat16)
    partner = passed(other, lambda c: c ^ 1)
    far = passed(mine, lambda c: c - 2 if c % 2 == 0 else c + 2)
    near = passed(jnp.concatenate([mine, partner], axis=0), lambda c: c + 2 if c % 2 == 0 else c - 2)
    held = (mine, partner, near, far)
    chosen = core.astype(jnp.int32).reshape(1)
    share = -(-USED // (GROUP * row_count)) * GROUP
    limit = pltpu.CompilerParams(vmem_limit_bytes=48 * 1024 * 1024)
    scalar = pl.BlockSpec(memory_space=pltpu.SMEM)
    vector = pl.BlockSpec(memory_space=pltpu.VMEM)
    packed, rows = pl.pallas_call(
        gram_kernel,
        out_shape=(
            jax.ShapeDtypeStruct((share * 3 // 2 * row_count, LANES), jnp.bfloat16),
            jax.ShapeDtypeStruct((SPAN, LANES, width), jnp.bfloat16),
        ),
        in_specs=[scalar] + [vector] * 4,
        out_specs=(vector, vector),
        compiler_params=limit,
        name="grams",
    )(chosen, *held)
    parts = packed.reshape(row_count, share * 3 // 2, LANES)
    parts = lax.all_to_all(parts, "row", split_axis=0, concat_axis=0, tiled=True)
    summed = restored(jnp.sum(parts.astype(jnp.float32), axis=0))
    copies = jnp.broadcast_to(summed[None], (row_count, share, LANES))
    whole = lax.all_to_all(copies, "row", split_axis=0, concat_axis=0, tiled=True)
    pair = jax.ShapeDtypeStruct((PAIR, width), jnp.bfloat16)
    kept, sent = pl.pallas_call(
        rounds_kernel,
        out_shape=(pair, pair),
        in_specs=[scalar, vector, vector],
        out_specs=(vector, vector),
        scratch_shapes=[pltpu.VMEM((SPAN - 1 - step, LANES, width), jnp.bfloat16) for step in range(ROUNDS - 1)],
        compiler_params=limit,
        name="rounds",
    )(chosen, whole.reshape(row_count * share, LANES), rows)
    got = passed(sent, lambda c: c ^ 1)
    return jnp.concatenate([jnp.where(core == 0, kept, got), jnp.where(core == 0, got, kept)], axis=0)


def solution(mesh):
    placed = (P(("col", "row"), None), P("col"))
    return jax.shard_map(
        on_device, mesh=mesh, in_specs=placed, out_specs=P("col", "row"), check_vma=False
    )
```

```python
import jax
import jax.numpy as jnp
from jax import lax
from jax.experimental import pallas as pl
from jax.experimental.pallas import tpu as pltpu
from jax.sharding import PartitionSpec as P

BLOCK = 48
PAIR = 2 * BLOCK
LANES = 128
ROUNDS = 4
SPAN = 5
CHUNK = LANES - PAIR

CROSS = [(s, t) for s in range(SPAN) for t in range(s + 1, min(s + ROUNDS, SPAN))]
LEFT, RIGHT = CROSS[:7], [(s, s) for s in range(SPAN)] + CROSS[7:]
HALF = LANES // 2
STEP = PAIR + BLOCK
USED = len(LEFT) * STEP
GROUP = 16


def iota(shape, dim):
    return lax.broadcasted_iota(jnp.int32, shape, dim)


def mm(a, b):
    return jnp.dot(a, b, preferred_element_type=jnp.float32)


def mm_nt(a, b):
    return lax.dot_general(a, b, (((1,), (1,)), ((), ())), preferred_element_type=jnp.float32)


def halves(value):
    high = value.astype(jnp.bfloat16)
    low = (value - high.astype(jnp.float32)).astype(jnp.bfloat16)
    return high, low


def shifted(value, lanes):
    return pltpu.roll(value, lanes % LANES, 1)


def fill(rows_ref, core, mine, partner, near, far):
    first = core[0] == 0
    pieces = [
        jnp.where(first, near[0:PAIR], far[...]),
        jnp.where(first, near[PAIR:], partner[...]),
        mine[...],
        jnp.where(first, partner[...], near[PAIR:]),
        jnp.where(first, far[...], near[0:PAIR]),
    ]
    for s in range(SPAN):
        rows_ref[s, 0:PAIR, :] = pieces[s]
        rows_ref[s, PAIR:, :] = jnp.zeros((CHUNK, mine.shape[1]), jnp.bfloat16)


def gram_kernel(core, mine, partner, near, far, packed, rows_ref):
    width = mine.shape[1]
    fill(rows_ref, core, mine, partner, near, far)
    block = {}
    for s in range(SPAN):
        end = min(s + ROUNDS, SPAN)
        others = rows_ref[s:end].reshape((end - s) * LANES, width)
        strip = mm_nt(rows_ref[s, 0:PAIR, :], others)
        for t in range(s, end):
            block[s, t] = strip[:, (t - s) * LANES : (t - s + 1) * LANES]
    lane = iota((PAIR, LANES), 1)
    short = lane[:BLOCK]
    flat = []
    for one, two in zip(LEFT, RIGHT):
        one, two = block[one], block[two]
        flat.append(jnp.where(lane < HALF, one, shifted(two, HALF)))
        first = jnp.where(short < CHUNK, shifted(one[:BLOCK], -HALF), shifted(one[BLOCK:], -CHUNK))
        second = jnp.where(short < PAIR, two[:BLOCK], shifted(two[BLOCK:], CHUNK))
        flat.append(jnp.where(short < HALF, first, second))
    groups = packed.shape[0] // (3 * GROUP // 2)
    flat.append(jnp.zeros((groups * GROUP - USED, LANES), jnp.float32))
    flat = jnp.concatenate(flat, axis=0)
    left = iota((GROUP // 2, LANES), 1) < HALF
    for pair in range(groups // 2):
        rows = []
        for at in (2 * pair * GROUP, (2 * pair + 1) * GROUP):
            value = flat[at : at + GROUP]
            lost = value - value.astype(jnp.bfloat16).astype(jnp.float32)
            lost = jnp.where(left, shifted(lost[: GROUP // 2], HALF), lost[GROUP // 2 :])
            rows += [value, lost]
        packed[3 * GROUP * pair : 3 * GROUP * (pair + 1), :] = jnp.concatenate(rows, axis=0).astype(jnp.bfloat16)


def restored(sums):
    sums = sums.reshape(-1, 3 * GROUP // 2, LANES)
    high, lost = sums[:, :GROUP], sums[:, GROUP:]
    lost = jnp.concatenate([lost[:, :, :HALF], lost[:, :, HALF:]], axis=1)
    return (high + jnp.pad(lost, ((0, 0), (0, 0), (HALF, 0)))).reshape(-1, LANES)


def unpacked(packed):
    lane = iota((PAIR, LANES), 1)
    floor = jnp.zeros((CHUNK, LANES), jnp.float32)
    gram = {}
    for k, (one, two) in enumerate(zip(LEFT, RIGHT)):
        main = packed[k * STEP : k * STEP + PAIR, :]
        rest = packed[k * STEP + PAIR : (k + 1) * STEP, :]
        sides = jnp.concatenate([shifted(rest, HALF), shifted(rest, CHUNK)], axis=0)
        gram[one] = jnp.where(lane < HALF, main, jnp.where(lane < PAIR, sides, 0.0))
        sides = jnp.concatenate([rest, shifted(rest, -CHUNK)], axis=0)
        gram[two] = jnp.where(lane < HALF, shifted(main, HALF), jnp.where(lane < PAIR, sides, 0.0))
    return {name: jnp.concatenate([value, floor], axis=0) for name, value in gram.items()}


def product(a, b):
    (ah, al), (bh, bl) = a, b
    value = mm(ah[:PAIR], bh) + (mm(al[:PAIR], bh) + mm(ah[:PAIR], bl))
    return jnp.concatenate([value, jnp.zeros((CHUNK, LANES), jnp.float32)], axis=0)


def turned_rotors(grams):
    shape = (LANES, LANES)
    row, lane = iota(shape, 0), iota(shape, 1)
    inside = (row < PAIR) & (lane < PAIR)
    eye = ((row == lane) & inside).astype(jnp.float32)
    terms = []
    for gram in grams:
        picked = gram * eye
        down = jnp.sum(picked, axis=1, keepdims=True)
        along = jnp.sum(picked, axis=0, keepdims=True)
        gap = along - down
        total = along + down
        bottom = gap * gap + 4.0 * gram * gram + 0.01 * total * total
        theta = gram * gap / jnp.where(inside, bottom, 1.0)
        terms.append(jnp.where(inside, theta, 0.0) * (-1.0 / 64.0))
    first = [halves(e) for e in terms]
    second = [product(a, a) for a in first]
    third = [product(halves(e2), a) for e2, a in zip(second, first)]
    result = []
    for e, e2, e3 in zip(terms, second, third):
        rest = e * (1.0 / 24.0) + e2 * (1.0 / 120.0) + e3 * (1.0 / 720.0)
        result.append(e + e2 * 0.5 + e3 * (1.0 / 6.0) + product(halves(e3), halves(rest)))
    for _ in range(6):
        split = [halves(d) for d in result]
        result = [2.0 * d + product(a, a) for d, a in zip(result, split)]
    return [(d + eye).astype(jnp.bfloat16) for d in result]


def turned_from_left(rows, value):
    high, low = halves(value)
    both = mm(rows, jnp.concatenate([high, low], axis=1))
    return both[:, :LANES] + both[:, LANES:]


def next_grams(gram, turned, count, reach):
    top_lane = iota((LANES, LANES), 1) < BLOCK
    top_half = iota((BLOCK, LANES), 1) < BLOCK
    floor = jnp.zeros((CHUNK, LANES), jnp.float32)
    right = {}
    for t in range(count):
        low = max(0, t - reach)
        stack = []
        for s in range(low, t + 1):
            stack += halves(gram[s, t])
        both = mm_nt(jnp.concatenate(stack, axis=0), turned[t])
        for s in range(low, t + 1):
            at = 2 * (s - low) * LANES
            right[s, t] = both[at : at + LANES] + both[at + LANES : at + 2 * LANES]
    following = {}
    for i in range(count - 1):
        upper, lower = turned[i][0:BLOCK], turned[i + 1][BLOCK:PAIR]
        for j in range(i, min(i + reach, count - 1)):
            top = turned_from_left(upper, jnp.where(top_lane, right[i, j], right[i, j + 1]))
            if i == j:
                bottom = turned_from_left(lower, right[i + 1, j + 1])
                empty = jnp.zeros((LANES - BLOCK, LANES), jnp.float32)
                mirrored = jnp.concatenate([top, empty], axis=0).T[BLOCK:PAIR]
                bottom = jnp.where(top_half, mirrored, bottom)
            else:
                bottom = turned_from_left(lower, jnp.where(top_lane, right[i + 1, j], right[i + 1, j + 1]))
            following[i, j] = jnp.concatenate([top, bottom, floor], axis=0)
    return following


def turn(rows, turned, i, into):
    old = rows[i]
    value = mm(turned[i][0:PAIR], old).astype(jnp.bfloat16)
    if i > 0:
        into[i - 1, BLOCK:PAIR, :] = value[BLOCK:]
    if i < into.shape[0]:
        into[i, 0:BLOCK, :] = value[:BLOCK]


def rounds_kernel(core, packed, rows_ref, kept, sent, *later):
    width = kept.shape[1]
    for ref in later:
        for i in range(ref.shape[0]):
            ref[i, PAIR:, :] = jnp.zeros((CHUNK, width), jnp.bfloat16)
    gram = unpacked(packed)
    rows = rows_ref
    for step in range(ROUNDS):
        count, reach = SPAN - step, ROUNDS - 1 - step
        turned = turned_rotors([gram[s, s] for s in range(count)])
        if reach == 0:
            break
        gram = next_grams(gram, turned, count, reach)
        for i in range(count):
            turn(rows, turned, i, later[step])
        rows = later[step]
    first = core[0] == 0
    ends = [mm(turned[i][0:PAIR], rows[i]).astype(jnp.bfloat16) for i in range(2)]
    kept[...] = jnp.where(first, ends[0], ends[1])
    sent[...] = jnp.where(first, ends[1], ends[0])


def passed(value, where):
    count = lax.axis_size("col")
    return lax.ppermute(value, "col", [(source, where(source) % count) for source in range(count)])


def on_device(frames, frame_order):
    row_count = lax.axis_size("row")
    width = frames.shape[1] // row_count
    core = lax.axis_index("col") % 2
    deep = width // LANES
    tiles = frames.reshape(-1, row_count, deep, LANES).transpose(1, 2, 0, 3)
    tiles = tiles.reshape(row_count, -1, LANES)
    arrived = lax.all_to_all(tiles, "row", split_axis=0, concat_axis=0, tiled=True)
    arrived = arrived.reshape(row_count, deep, -1, LANES).transpose(0, 2, 1, 3)
    arrived = arrived.reshape(frame_order.shape[0], width)
    order = jnp.where(core == 0, jnp.roll(frame_order, PAIR), frame_order)
    picks = (order[:, None] == iota((1, order.shape[0]), 1)).astype(jnp.bfloat16)
    mine = mm(picks[:PAIR], arrived).astype(jnp.bfloat16)
    other = mm(picks[PAIR:], arrived).astype(jnp.bfloat16)
    partner = passed(other, lambda c: c ^ 1)
    far = passed(mine, lambda c: c - 2 if c % 2 == 0 else c + 2)
    near = passed(jnp.concatenate([mine, partner], axis=0), lambda c: c + 2 if c % 2 == 0 else c - 2)
    held = (mine, partner, near, far)
    chosen = core.astype(jnp.int32).reshape(1)
    share = -(-USED // (GROUP * row_count)) * GROUP
    limit = pltpu.CompilerParams(vmem_limit_bytes=48 * 1024 * 1024)
    scalar = pl.BlockSpec(memory_space=pltpu.SMEM)
    vector = pl.BlockSpec(memory_space=pltpu.VMEM)
    packed, rows = pl.pallas_call(
        gram_kernel,
        out_shape=(
            jax.ShapeDtypeStruct((share * 3 // 2 * row_count, LANES), jnp.bfloat16),
            jax.ShapeDtypeStruct((SPAN, LANES, width), jnp.bfloat16),
        ),
        in_specs=[scalar] + [vector] * 4,
        out_specs=(vector, vector),
        compiler_params=limit,
        name="grams",
    )(chosen, *held)
    parts = packed.reshape(row_count, share * 3 // 2, LANES)
    parts = lax.all_to_all(parts, "row", split_axis=0, concat_axis=0, tiled=True)
    summed = restored(jnp.sum(parts.astype(jnp.float32), axis=0))
    copies = jnp.broadcast_to(summed[None], (row_count, share, LANES))
    whole = lax.all_to_all(copies, "row", split_axis=0, concat_axis=0, tiled=True)
    pair = jax.ShapeDtypeStruct((PAIR, width), jnp.bfloat16)
    kept, sent = pl.pallas_call(
        rounds_kernel,
        out_shape=(pair, pair),
        in_specs=[scalar, vector, vector],
        out_specs=(vector, vector),
        scratch_shapes=[pltpu.VMEM((SPAN - 1 - step, LANES, width), jnp.bfloat16) for step in range(ROUNDS - 1)],
        compiler_params=limit,
        name="rounds",
    )(chosen, whole.reshape(row_count * share, LANES), rows)
    got = passed(sent, lambda c: c ^ 1)
    return jnp.concatenate([jnp.where(core == 0, kept, got), jnp.where(core == 0, got, kept)], axis=0)


def solution(mesh):
    placed = (P(("col", "row"), None), P("col"))
    return jax.shard_map(
        on_device, mesh=mesh, in_specs=placed, out_specs=P("col", "row"), check_vma=False
    )
```
